32 devices in a mesh: groups: 2 (over y), expert: 16 (over z, x, core), tensor: 1.
Axes of the slice: x: 2, y: 2, z: 4, core: 2. Of those that a mesh axis runs over, the one named last changes fastest.
Arguments:
- tokens: bfloat16 [4096, 3072], P(('groups', 'expert')), parts along dimension 0, may hold values from -6 to 6
- lengths: int32 [32], P(('groups', 'expert')), parts along dimension 0, may hold values from 32 to 128, as said below
- routed_expert: int32 [4096, 1], P(('groups', 'expert')), parts along dimension 0, may hold values from 0 to 1; in each aligned block of 128 rows (0 to 127, 128 to 255, ...) at most 80 rows name the same one
- attention_gain: float32 [3072], replicated, may hold values from 0.1 to 1.9
- w_query: bfloat16 [3072, 256], P('expert', 'tensor'), may hold values from -0.108253175 to 0.108253175
- w_key: bfloat16 [3072, 256], P('expert', 'tensor'), may hold values from -0.108253175 to 0.108253175
- w_value: bfloat16 [3072, 256], P('expert', 'tensor'), may hold values from -0.109375 to 0.109375
- w_out: bfloat16 [3072, 256], P('expert', 'tensor'), may hold values from -0.375 to 0.375
- expert_gain: float32 [3072], replicated, may hold values from 0.1 to 1.9
- w_gate: bfloat16 [3072, 16384], P(None, ('expert', 'tensor')), may hold values from -0.109375 to 0.109375
- w_up: bfloat16 [3072, 16384], P(None, ('expert', 'tensor')), may hold values from -0.109375 to 0.109375
- w_down: bfloat16 [16384, 3072], P(('expert', 'tensor')), may hold values from -0.0625 to 0.0625
Outputs:
- output: bfloat16 [4096, 3072], P(('groups', 'expert'), 'tensor'), parts along dimension 0
The draws below stay inside these ranges and needn't reach their ends.
There are 2 independent parts, one for each index of `groups`. The reference program is written for one: setup_inputs(seed, part) draws one part's arguments, and reference() takes and returns one part's arrays. A program takes and returns all parts, laid end to end along the dimension named above; an argument that names none is the same for every part. Nothing has to cross between parts.
Inputs may be any that keep to these rules, and one draw needn't show every extreme that they name: `routed_expert`: in each aligned block of the 128 rows of one sequence, no expert is named by more than 80 rows, a bound that some block reaches. `lengths`: some sequence has all 128 positions valid, and some has the fewest that any sequence may have.
All inputs are finite; a program needn't handle non-finite values.
Results may differ from the reference program's by a relative error of at most 0.015.
Values may be sent and summed in bfloat16 or wider, within the bound.
A program may use at most 128 MiB of HBM per device.

```python
import math
import jax
import jax.numpy as jnp
import numpy as np
from jax import lax

D = 3072
HEAD = 128
HEADS = 2
FF = 8192
GROUP = 8
TOK_DEV = 128
EXPERTS = 2
SEQS = 16
TOKENS = 2048
CAP = 80
N_EXPERT = 16


def draw_lengths(key, part):
    key = jax.random.fold_in(key, 11)
    first_key, second_key = jax.random.split(key)
    lowest = max(1, TOK_DEV // 4)
    drawn = jax.random.randint(first_key, (SEQS,), lowest, TOK_DEV + 1)
    placing = jax.random.permutation(second_key, SEQS)
    drawn = jnp.where(placing == 0, TOK_DEV, drawn)
    drawn = jnp.where(placing == 1, lowest, drawn)
    return drawn.astype(jnp.int32)


def draw_tokens(key, part):
    key = jax.random.fold_in(key, 21)
    noise_key = jax.random.fold_in(key, 0)
    noise = jax.random.normal(noise_key, (TOKENS, D), jnp.float32)
    return jnp.clip(noise, -6.0, 6.0).astype(jnp.bfloat16)


def draw_w_query(key, part):
    key = jax.random.fold_in(key, 31)
    base = jax.random.normal(key, (D, HEADS * HEAD), jnp.float32)
    return (jnp.clip(base, -5.9, 5.9) * D ** (-0.5)).astype(jnp.bfloat16)


def draw_w_key(key, part):
    key = jax.random.fold_in(key, 41)
    base = jax.random.normal(key, (D, HEADS * HEAD), jnp.float32)
    return (jnp.clip(base, -5.9, 5.9) * D ** (-0.5)).astype(jnp.bfloat16)


def block_scale(rng, extent, cuts, low, high):
    gain = 1.0
    for dim, blocks in cuts:
        heights = jax.random.uniform(jax.random.fold_in(jax.random.fold_in(rng, 6), dim), (blocks,), jnp.float32, low / len(cuts), high / len(cuts))
        gain = gain * jnp.repeat(jnp.exp(heights), extent[dim] // blocks).reshape((-1,) + (1,) * (len(extent) - 1 - dim))
    return gain


def assign_block(rng, own, number, rows, amount, top, bound, slope):
    order = jax.random.permutation(rng, amount)
    crowded, usual = portions_of(amount, rows * top, bound, slope, True), portions_of(amount, rows * top, bound, slope, False)
    places = jnp.arange(amount)

    def named(sizes, offset_by):
        used = int((sizes > 0).sum())
        fixed = max(1, used // 4)
        shifted = fixed + (places - fixed + offset_by * (used - fixed)) % max(1, amount - fixed)
        return jnp.zeros((amount,), jnp.int32).at[order[jnp.where(places < fixed, places, shifted)]].set(jnp.asarray(sizes, jnp.int32))

    sizes = jnp.where(number % 4 == 0, named(crowded, number // 4), named(usual, number - number // 4 - 1))
    mixed = jax.random.permutation(jax.random.fold_in(own, 3), amount)
    donor, sink = mixed[0:amount // 2 * 2:2], mixed[1:amount // 2 * 2:2]
    margin = jnp.minimum(sizes[donor] - 1, bound - sizes[sink]) // 2
    margin = jnp.where((donor == order[0]) | (sink == order[0]) | (sizes[sink] == 0), 0, jnp.maximum(margin, 0))
    shifted = jax.random.randint(jax.random.fold_in(own, 4), (amount // 2,), 0, 1 << 20) % (margin + 1)
    sizes = sizes.at[donor].add(-shifted).at[sink].add(shifted)
    items = jnp.searchsorted(jnp.cumsum(sizes), jnp.arange(rows * top), side="right").astype(jnp.int32)
    grid = items.reshape(top, rows).T
    grid = grid[jax.random.permutation(jax.random.fold_in(own, 1), rows)]
    offset_by = jax.random.randint(jax.random.fold_in(own, 2), (rows, 1), 0, top)
    return jnp.take_along_axis(grid, (jnp.arange(top)[None, :] + offset_by) % top, axis=1)


def portions_of(amount, total, limit, slope, full):
    weights = [(1 << 20) // math.isqrt(grade ** slope) + 1 for grade in range(1, amount + 1)]
    largest = limit if full else min(limit, max(-(-total // amount), total * weights[0] // sum(weights)))
    least = 1 if total - largest >= amount - 1 else 0
    counts, spare = [largest] + [least] * (amount - 1), total - largest - least * (amount - 1)
    while spare > 0:
        free = [i for i in range(1, amount) if counts[i] < largest] or [i for i in range(1, amount) if counts[i] < limit]
        mass, remaining = sum([weights[i] for i in free]), spare
        for i in free:
            extra = min(limit - counts[i], max(1, remaining * weights[i] // mass), spare)
            counts[i] = counts[i] + extra
            spare = spare - extra
    return np.array(counts)


def normal_values(stream_key, shape, scale, reach, pieces=(), kind=jnp.bfloat16):
    factor_of = block_scale(stream_key, shape, pieces, -0.22, 0.18) if pieces else 1.0
    entries = jax.random.normal(stream_key, shape, jnp.float32) * scale * factor_of
    return jnp.minimum(jnp.maximum(entries, -reach), reach).astype(kind)


def setup_inputs(seed: int = 0, part: int = 0) -> dict:
    key_of = jax.random.split(jax.random.key(seed), 13)
    part_splits = jax.random.split(jax.random.fold_in(key_of[12], part), 13)
    tokens = draw_tokens(jax.random.fold_in(jax.random.fold_in(key_of[12], part), 71), part)
    lengths = draw_lengths(jax.random.fold_in(jax.random.fold_in(key_of[12], part), 71), part)
    routed_expert_keys = jax.random.split(jax.random.fold_in(part_splits[2], 1), TOKENS // TOK_DEV)
    routed_expert_turns = jax.random.permutation(jax.random.fold_in(part_splits[2], 3), TOKENS // TOK_DEV)
    routed_expert = jax.vmap(lambda own, number: assign_block(jax.random.fold_in(part_splits[2], 2), own, number, TOK_DEV, EXPERTS, 1, CAP, 1))(routed_expert_keys, routed_expert_turns).reshape((TOKENS, 1))
    attention_gain = jnp.clip(1.0 + 0.18 * jax.random.normal(key_of[3], (D,), jnp.float32), 0.1, 1.9)
    w_query = draw_w_query(jax.random.fold_in(key_of[12], 71), part)
    w_key = draw_w_key(jax.random.fold_in(key_of[12], 71), part)
    w_value = normal_values(key_of[6], (D, HEADS * HEAD), D ** -0.5, 0.109375, ((0, 16),))
    w_out = normal_values(key_of[7], (D, HEADS * HEAD), (HEADS * HEAD) ** -0.5, 0.375, ((0, 16),))
    expert_gain = jnp.clip(1.0 + 0.18 * jax.random.normal(key_of[8], (D,), jnp.float32), 0.1, 1.9)
    w_gate = normal_values(key_of[9], (D, EXPERTS * FF), D ** -0.5, 0.109375, ((1, 16),))
    w_up = normal_values(key_of[10], (D, EXPERTS * FF), D ** -0.5, 0.109375, ((1, 16),))
    w_down = normal_values(key_of[11], (EXPERTS * FF, D), FF ** -0.5, 0.0625, ((0, 16),))
    return {"tokens": tokens, "lengths": lengths, "routed_expert": routed_expert, "attention_gain": attention_gain, "w_query": w_query, "w_key": w_key, "w_value": w_value, "w_out": w_out, "expert_gain": expert_gain, "w_gate": w_gate, "w_up": w_up, "w_down": w_down}


def rms_scale(values, gain_vector):
    widened = values.astype(jnp.float32)
    mean_square = lax.optimization_barrier(jnp.mean(widened * widened, axis=-1, keepdims=True))
    return (widened * lax.rsqrt(mean_square + 1e-05) * gain_vector).astype(jnp.bfloat16)

def reference(tokens, lengths, routed_expert, attention_gain, w_query, w_key, w_value, w_out, expert_gain, w_gate, w_up, w_down):
    normed = rms_scale(tokens, attention_gain)
    seq_shape = (SEQS, TOK_DEV, HEADS, HEAD)
    query_rows = jnp.dot(normed, w_query, preferred_element_type=jnp.float32).astype(jnp.bfloat16)
    key_rows = jnp.dot(normed, w_key, preferred_element_type=jnp.float32).astype(jnp.bfloat16)
    value_rows = jnp.dot(normed, w_value, preferred_element_type=jnp.float32).astype(jnp.bfloat16)
    scores = jnp.einsum('sqhd,skhd->shqk', query_rows.reshape(seq_shape).astype(jnp.float32), key_rows.reshape(seq_shape).astype(jnp.float32)) * HEAD ** (-0.5)
    positions = jnp.arange(TOK_DEV, dtype=jnp.int32)
    causal = (positions[None, :] <= positions[:, None])[None, None]
    valid = positions[None, None, None, :] < lengths[:, None, None, None]
    scores = jnp.where(causal & valid, scores, -1e+30)
    weights = jax.nn.softmax(scores, axis=-1).astype(jnp.bfloat16)
    context = jnp.einsum('shqk,skhd->sqhd', weights.astype(jnp.float32), value_rows.reshape(seq_shape).astype(jnp.float32)).astype(jnp.bfloat16)
    context = context.reshape(TOKENS, HEADS * HEAD)
    attended = jnp.dot(context, w_out.T, preferred_element_type=jnp.float32)
    after_attention = (tokens.astype(jnp.float32) + attended).astype(jnp.bfloat16)
    expert_input = rms_scale(after_attention, expert_gain)
    chosen = routed_expert[:, 0].reshape(N_EXPERT, TOK_DEV)
    one_hot = (chosen[:, :, None] == jnp.arange(EXPERTS, dtype=jnp.int32)[None, None, :]).astype(jnp.int32)
    within = lax.optimization_barrier(jnp.sum((jnp.cumsum(one_hot, axis=1) - 1) * one_hot, axis=2))
    source = jnp.arange(N_EXPERT, dtype=jnp.int32)[:, None]
    target = (chosen * (N_EXPERT * CAP) + source * CAP + within).reshape(TOKENS).astype(jnp.int32)
    buffer_rows = jnp.zeros((EXPERTS * N_EXPERT * CAP, D), jnp.bfloat16).at[target].set(expert_input)
    buffer_rows = buffer_rows.reshape(EXPERTS, N_EXPERT * CAP, D)
    part_width = FF // GROUP

    def run_expert(operands):
        arrived, number = operands
        start = (number * FF).astype(jnp.int32)
        gate_weight = lax.dynamic_slice_in_dim(w_gate, start, FF, 1)
        up_weight = lax.dynamic_slice_in_dim(w_up, start, FF, 1)
        down_weight = lax.dynamic_slice_in_dim(w_down, start, FF, 0)
        gate_sum = jnp.dot(arrived, gate_weight, preferred_element_type=jnp.float32)
        upward = jnp.dot(arrived, up_weight, preferred_element_type=jnp.float32)
        hidden = (jax.nn.silu(gate_sum) * upward).astype(jnp.bfloat16)
        total = jnp.zeros((arrived.shape[0], D), jnp.float32)
        for part in range(GROUP):
            lower = part * part_width
            piece = jnp.dot(hidden[:, lower:lower + part_width], down_weight[lower:lower + part_width], preferred_element_type=jnp.float32).astype(jnp.bfloat16)
            total = total + piece.astype(jnp.float32)
        return total
    outputs = lax.map(run_expert, (buffer_rows, jnp.arange(EXPERTS, dtype=jnp.int32)))
    expert_rows = outputs.reshape(EXPERTS * N_EXPERT * CAP, D)[target]
    return (after_attention.astype(jnp.float32) + expert_rows).astype(jnp.bfloat16)
```

```python
import functools

import jax
import jax.numpy as jnp
from jax import lax
from jax.experimental import pallas as pl
from jax.experimental.pallas import tpu as pltpu
from jax.sharding import PartitionSpec as P

HEAD = 128
GROUP = 8


def rms_scale(values, gain_vector):
    widened = values.astype(jnp.float32)
    mean_square = jnp.mean(widened * widened, axis=-1, keepdims=True)
    return (widened * lax.rsqrt(mean_square + 1e-05) * gain_vector).astype(jnp.bfloat16)


def slot_numbers(routed, experts, capacity):
    chosen = routed[:, 0]
    one_hot = (chosen[:, None] == jnp.arange(experts, dtype=jnp.int32)[None, :]).astype(jnp.int32)
    running = jnp.cumsum(one_hot, axis=0) - 1
    within = jnp.sum(running * one_hot, axis=1)
    return chosen * capacity + within


def attend(query_rows, key_rows, value_rows, length):
    token_count = query_rows.shape[0]
    head_shape = (token_count, query_rows.shape[1] // HEAD, HEAD)
    scores = jnp.einsum(
        "qhd,khd->hqk",
        query_rows.reshape(head_shape),
        key_rows.reshape(head_shape),
        preferred_element_type=jnp.float32,
    ) * HEAD ** (-0.5)
    positions = jnp.arange(token_count, dtype=jnp.int32)
    allowed = (positions[None, :] <= positions[:, None]) & (positions[None, :] < length)
    scores = jnp.where(allowed[None], scores, -1e30)
    weights = jax.nn.softmax(scores, axis=-1).astype(jnp.bfloat16)
    context = jnp.einsum(
        "hqk,khd->qhd", weights, value_rows.reshape(head_shape), preferred_element_type=jnp.float32
    ).astype(jnp.bfloat16)
    return context.reshape(token_count, -1)


def swiglu_part(arrived_block, gate_weight, up_weight, down_weight):
    gate_sum = jnp.einsum(
        "scd,df->scf", arrived_block, gate_weight, preferred_element_type=jnp.float32
    )
    upward = jnp.einsum("scd,df->scf", arrived_block, up_weight, preferred_element_type=jnp.float32)
    hidden = (jax.nn.silu(gate_sum) * upward).astype(jnp.bfloat16)
    return jnp.einsum("scf,fd->scd", hidden, down_weight, preferred_element_type=jnp.float32)


def body(
    tokens,
    lengths,
    routed_expert,
    attention_gain,
    w_query,
    w_key,
    w_value,
    w_out,
    expert_gain,
    w_gate,
    w_up,
    w_down,
):
    token_count = tokens.shape[0]
    model_width = tokens.shape[1]
    normed = rms_scale(tokens, attention_gain)
    query_sum = jnp.dot(
        normed,
        lax.all_gather(w_query, "expert", axis=0, tiled=True),
        preferred_element_type=jnp.float32,
    )
    key_sum = jnp.dot(
        normed,
        lax.all_gather(w_key, "expert", axis=0, tiled=True),
        preferred_element_type=jnp.float32,
    )
    value_sum = jnp.dot(
        normed,
        lax.all_gather(w_value, "expert", axis=0, tiled=True),
        preferred_element_type=jnp.float32,
    )
    context = attend(
        query_sum.astype(jnp.bfloat16),
        key_sum.astype(jnp.bfloat16),
        value_sum.astype(jnp.bfloat16),
        lengths[0],
    )
    partial_out = lax.dot_general(
        context,
        lax.all_gather(w_out, "expert", axis=0, tiled=True),
        (((1,), (1,)), ((), ())),
        preferred_element_type=jnp.float32,
    )
    cores = lax.axis_size("tensor")
    core_index = lax.axis_index("tensor")
    summed = lax.psum(partial_out, "tensor")
    after_attention = (tokens.astype(jnp.float32) + summed).astype(jnp.bfloat16)
    expert_input = rms_scale(after_attention, expert_gain)
    devices_along = lax.axis_size("expert")
    expert_count = devices_along // GROUP
    capacity = min(token_count, 2 * max(1, 5 * token_count // (8 * expert_count)))
    slot_ids = slot_numbers(routed_expert, expert_count, capacity)
    outgoing_all = (
        jnp.zeros((expert_count * capacity, model_width), jnp.bfloat16)
        .at[slot_ids]
        .set(expert_input)
    )
    outgoing_all = jnp.repeat(
        outgoing_all.reshape(expert_count, capacity, model_width), GROUP, axis=0
    )
    half_width = model_width // cores
    arrived = swiglu_part(
        lax.all_to_all(outgoing_all, "expert", split_axis=0, concat_axis=0, tiled=True),
        w_gate,
        w_up,
        w_down,
    )
    reduced = lax.psum_scatter(arrived, "tensor", scatter_dimension=2, tiled=True).astype(
        jnp.bfloat16
    )
    returned = lax.all_to_all(reduced, "expert", split_axis=0, concat_axis=0, tiled=True)
    part_sums = returned.reshape(expert_count, GROUP, capacity, half_width).astype(jnp.float32)
    expert_rows = jnp.sum(part_sums, axis=1).reshape(expert_count * capacity, half_width)[slot_ids]
    after_half = lax.dynamic_slice_in_dim(after_attention, core_index * half_width, half_width, 1)
    return (after_half.astype(jnp.float32) + expert_rows).astype(jnp.bfloat16)


BF16 = jnp.bfloat16
F32 = jnp.float32
VMEM_BYTES = 60 * 1024 * 1024
TILES = 4


def remote(src, dst, send, recv, target):
    return pltpu.make_async_remote_copy(
        src_ref=src,
        dst_ref=dst,
        send_sem=send,
        recv_sem=recv,
        device_id={"expert": target},
        device_id_type=pl.DeviceIdType.MESH,
    )


def greet(targets):
    barrier = pltpu.get_barrier_semaphore()
    for target in targets:
        pl.semaphore_signal(
            barrier, inc=1, device_id={"expert": target}, device_id_type=pl.DeviceIdType.MESH
        )
    pl.semaphore_wait(barrier, len(targets))


def place():
    me = lax.axis_index("expert")
    core = me % 2
    x = (me // 2) % 2
    z = me // 4
    return me, core, x, z


def gather_kernel(
    lengths, tokens, w_qkv, w_out, gain, egain, after, ein, qkv_full, out_full, normed, ctx, send, recv, local
):
    me, core, x, z = place()
    shard = w_out.shape[0]
    sib = me + 1 - 2 * core
    across = me + 2 - 4 * x
    def rows(who):
        return pl.ds(pl.multiple_of(who * shard, 64), shard)

    fulls = (qkv_full, out_full)
    copies = []
    for g, own in enumerate((w_qkv, w_out)):
        copy = pltpu.make_async_copy(own, fulls[g].at[rows(me)], local.at[g])
        copy.start()
        copies.append(copy)
    wide = tokens[...].astype(F32)
    mean_square = jnp.mean(wide * wide, axis=-1, keepdims=True)
    normed[...] = (wide * lax.rsqrt(mean_square + 1e-05) * gain[...]).astype(BF16)
    for copy in copies:
        copy.wait()
    greet((sib, across, (me + 4) % 16, (me + 12) % 16))

    targets = (me + 4, me - 4, across, sib)

    def move(g, direction, who):
        block = fulls[g].at[rows(who)]
        return remote(block, block, send.at[g, direction, who], recv.at[g, who], targets[direction])

    def arrived(g, who):
        block = fulls[g].at[rows(who)]
        remote(block, block, send.at[g, 0, who], recv.at[g, who], sib).wait_recv()

    def each_up(who, act, g):
        @pl.when(z < 3)
        def _():
            act(move(g, 0, who))

    def each_down(who, act, g):
        @pl.when(z > 0)
        def _():
            act(move(g, 1, who))

    def start(copy):
        copy.start()

    def finish(copy):
        copy.wait_send()

    def column(g, act, wait):
        each_up(me, act, g)
        each_down(me, act, g)
        act(move(g, 2, me))
        act(move(g, 3, me))
        for d in (1, 2, 3):

            @pl.when(z >= d)
            def _():
                who = me - 4 * d
                if wait:
                    arrived(g, who)
                each_up(who, act, g)
                act(move(g, 2, who))
                act(move(g, 3, who))

            @pl.when(z + d <= 3)
            def _():
                who = me + 4 * d
                if wait:
                    arrived(g, who)
                each_down(who, act, g)
                act(move(g, 2, who))
                act(move(g, 3, who))

        def pass_on(who):
            if wait:
                arrived(g, who)
            act(move(g, 3, who))

        pass_on(across)
        for d in (1, 2, 3):

            @pl.when(z >= d)
            def _():
                pass_on(across - 4 * d)

            @pl.when(z + d <= 3)
            def _():
                pass_on(across + 4 * d)

    def siblings(g):
        for zz in range(4):
            for xx in range(2):
                arrived(g, (zz * 2 + xx) * 2 + 1 - core)

    column(0, start, True)
    column(1, start, True)
    siblings(0)

    width = qkv_full.shape[1] // 3
    qkv = jnp.dot(normed[...], qkv_full[...], preferred_element_type=F32).astype(BF16)
    count = tokens.shape[0]
    qpos = lax.broadcasted_iota(jnp.int32, (count, count), 0)
    kpos = lax.broadcasted_iota(jnp.int32, (count, count), 1)
    allowed = (kpos <= qpos) & (kpos < lengths[...])
    for head in range(width // HEAD):
        at = head * HEAD
        query = qkv[:, at : at + HEAD]
        key = qkv[:, width + at : width + at + HEAD]
        value = qkv[:, 2 * width + at : 2 * width + at + HEAD]
        scores = lax.dot_general(
            query, key, (((1,), (1,)), ((), ())), preferred_element_type=F32
        ) * HEAD ** (-0.5)
        scores = jnp.where(allowed, scores, -1e30)
        peak = jnp.max(scores, axis=-1, keepdims=True)
        weights = jnp.exp(scores - peak)
        weights = (weights / jnp.sum(weights, axis=-1, keepdims=True)).astype(BF16)
        ctx[:, at : at + HEAD] = jnp.dot(weights, value, preferred_element_type=F32).astype(BF16)
    siblings(1)
    attended = lax.dot_general(
        ctx[...], out_full[...], (((1,), (1,)), ((), ())), preferred_element_type=F32
    )
    after[...] = (tokens[...].astype(F32) + attended).astype(BF16)
    wide = after[...].astype(F32)
    mean_square = jnp.mean(wide * wide, axis=-1, keepdims=True)
    ein[...] = (wide * lax.rsqrt(mean_square + 1e-05) * egain[...]).astype(BF16)
    column(0, finish, False)
    column(1, finish, False)


def expert_kernel(
    half_a,
    ein,
    after,
    perm,
    perm_t,
    w_gate,
    w_up,
    w_down,
    out,
    gate_v,
    up_v,
    down_v,
    rows_in,
    far_own,
    hidden,
    part,
    from_sib,
    diag_x,
    diag_z,
    sum_x,
    sum_z,
    near_sum,
    far_sum,
    far_back,
    wsem,
    gsend,
    grecv,
    csem,
    rsend,
    rrecv,
    fsend,
    frecv,
):
    me, core, x, z = place()
    near = z // 2
    sib = me + 1 - 2 * core
    across = me + 2 - 4 * x
    along = me + 4 - 8 * (z % 2)
    mirror = me + 8 - 16 * near
    slots, cap, width = rows_in.shape[1], rows_in.shape[2], rows_in.shape[3]
    loads = []
    for k, (src, dst) in enumerate(((w_gate, gate_v), (w_up, up_v), (w_down, down_v))):
        copy = pltpu.make_async_copy(src, dst, wsem.at[k])
        copy.start()
        loads.append(copy)
    far_own[...] = jnp.dot(perm[1 - near], ein[...], preferred_element_type=F32).astype(BF16)
    rows_in[0, 0] = jnp.dot(perm[near], ein[...], preferred_element_type=F32).astype(BF16)
    greet((sib, across, along, mirror))

    started = []

    def go(copy):
        copy.start()
        started.append(copy)
        return copy

    def gather_own(k):
        own = rows_in.at[k, 0]
        to_x = go(remote(own, rows_in.at[k, 1], gsend.at[k, 0], grecv.at[k, 0], across))
        to_z = go(remote(own, rows_in.at[k, 2], gsend.at[k, 1], grecv.at[k, 1], along))
        to_s = go(remote(own, rows_in.at[k, 4], gsend.at[k, 2], grecv.at[k, 2], sib))
        return to_x, to_z, to_s

    def gather_pass(k, first):
        first[0].wait_recv()
        from_x = rows_in.at[k, 1]
        rest = cap - half_a
        d_z = go(
            remote(
                from_x.at[pl.ds(half_a, rest)],
                rows_in.at[k, 3, pl.ds(half_a, rest)],
                gsend.at[k, 3],
                grecv.at[k, 3],
                along,
            )
        )
        s1 = go(remote(from_x, rows_in.at[k, 5], gsend.at[k, 4], grecv.at[k, 4], sib))
        first[1].wait_recv()
        from_z = rows_in.at[k, 2]
        d_x = go(
            remote(
                from_z.at[pl.ds(0, half_a)],
                rows_in.at[k, 3, pl.ds(0, half_a)],
                gsend.at[k, 5],
                grecv.at[k, 5],
                across,
            )
        )
        s2 = go(remote(from_z, rows_in.at[k, 6], gsend.at[k, 6], grecv.at[k, 6], sib))
        return d_z, d_x, s1, s2

    def gather_last(k, second):
        second[0].wait_recv()
        second[1].wait_recv()
        return go(
            remote(rows_in.at[k, 3], rows_in.at[k, 7], gsend.at[k, 7], grecv.at[k, 7], sib)
        )

    def gather_done(first, second, third):
        first[2].wait_recv()
        second[2].wait_recv()
        second[3].wait_recv()
        third.wait_recv()

    fan = gate_v.shape[1] // TILES
    tile = width // TILES

    def up_tile(k, t):
        cols = pl.ds(pl.multiple_of(t * fan, fan), fan)
        given = rows_in[k].reshape(slots * cap, width)
        gate = jnp.dot(given, gate_v[:, cols], preferred_element_type=F32)
        upward = jnp.dot(given, up_v[:, cols], preferred_element_type=F32)
        hidden[:, cols] = (jax.nn.silu(gate) * upward).astype(BF16)

    def down_tile(k, t):
        cols = pl.ds(pl.multiple_of(t * tile, tile), tile)
        total = jnp.dot(hidden[...], down_v[:, cols], preferred_element_type=F32)
        part[k * TILES + t] = total.astype(BF16).reshape(slots, cap, tile)

    def summing(kind, i):
        rest = cap - half_a
        ends = (
            (part.at[i, pl.ds(4, 4)], from_sib.at[i], sib),
            (part.at[i, 3, pl.ds(0, half_a)], diag_x.at[i], across),
            (part.at[i, 3, pl.ds(half_a, rest)], diag_z.at[i], along),
            (part.at[i, 1], sum_x.at[i], across),
            (part.at[i, 2], sum_z.at[i], along),
        )[kind]
        return remote(ends[0], ends[1], rsend.at[kind, i], rrecv.at[kind, i], ends[2])

    def plus(a, b):
        return (a.astype(F32) + b.astype(F32)).astype(BF16)

    def step_core(i):
        summing(0, i).wait_recv()
        part[i, 3] = plus(part[i, 3], from_sib[i, 3])
        summing(1, i).start()
        summing(2, i).start()
        part[i, 0:3] = plus(part[i, 0:3], from_sib[i, 0:3])

    def step_diag(i):
        summing(1, i).wait_recv()
        part[i, 2, 0:half_a] = plus(part[i, 2, 0:half_a], diag_x[i])
        summing(4, i).start()
        summing(2, i).wait_recv()
        part[i, 1, half_a:cap] = plus(part[i, 1, half_a:cap], diag_z[i])
        summing(3, i).start()

    def total_of(i):
        summing(3, i).wait_recv()
        summing(4, i).wait_recv()
        total = part[i, 0].astype(F32) + sum_x[i].astype(F32) + sum_z[i].astype(F32)
        return total.astype(BF16)

    def returning(t):
        return remote(far_sum.at[t], far_back.at[t], fsend.at[t], frecv.at[t], mirror)

    def loop(body):
        lax.fori_loop(0, TILES, lambda t, c: (body(t), c)[1], 0)

    near_first = gather_own(0)
    crossing = go(remote(far_own, rows_in.at[1, 0], csem.at[0], csem.at[1], mirror))
    near_second = gather_pass(0, near_first)
    near_third = gather_last(0, near_second)
    crossing.wait_recv()
    far_first = gather_own(1)
    gather_done(near_first, near_second, near_third)
    for copy in loads:
        copy.wait()
    loop(functools.partial(up_tile, 0))
    far_second = gather_pass(1, far_first)

    def near_down(t):
        down_tile(0, t)
        summing(0, t).start()

        @pl.when(t > 0)
        def _():
            step_core(t - 1)

    loop(near_down)
    step_core(TILES - 1)
    far_third = gather_last(1, far_second)
    gather_done(far_first, far_second, far_third)

    def far_up(t):
        up_tile(1, t)
        step_diag(t)

    loop(far_up)

    def far_down(t):
        i = TILES + t
        down_tile(1, t)
        summing(0, i).start()

        @pl.when(t > 0)
        def _():
            step_core(i - 1)

        near_sum[t] = total_of(t)

    loop(far_down)
    step_core(2 * TILES - 1)
    loop(lambda t: step_diag(TILES + t))

    def far_total(t):
        far_sum[t] = total_of(TILES + t)
        returning(t).start()

    loop(far_total)

    def finish(t):
        cols = pl.ds(pl.multiple_of(t * tile, tile), tile)
        returning(t).wait_recv()
        moved = jnp.dot(perm_t[near], near_sum[t], preferred_element_type=F32)
        moved = moved + jnp.dot(perm_t[1 - near], far_back[t], preferred_element_type=F32)
        out[:, cols] = (after[:, cols].astype(F32) + moved).astype(BF16)
        returning(t).wait_send()

    loop(finish)
    for copy in started:
        copy.wait_send()

    def drain(i, c):
        for kind in range(5):
            summing(kind, i).wait_send()
        return c

    lax.fori_loop(0, 2 * TILES, drain, 0)


def fast_body(
    tokens,
    lengths,
    routed_expert,
    attention_gain,
    w_query,
    w_key,
    w_value,
    w_out,
    expert_gain,
    w_gate,
    w_up,
    w_down,
):
    count, width = tokens.shape
    devices = lax.axis_size("expert")
    experts = devices // GROUP
    capacity = min(count, 2 * max(1, 5 * count // (8 * experts)))
    vmem = pl.BlockSpec(memory_space=pltpu.VMEM)
    anywhere = pl.BlockSpec(memory_space=pl.ANY)
    heads = w_query.shape[1]
    w_qkv = jnp.concatenate([w_query, w_key, w_value], axis=1)
    dma = pltpu.SemaphoreType.DMA
    after, ein = pl.pallas_call(
        gather_kernel,
        out_shape=[jax.ShapeDtypeStruct((count, width), BF16)] * 2,
        in_specs=[vmem] * 6,
        out_specs=[vmem] * 2,
        scratch_shapes=[
            pltpu.VMEM((width, 3 * heads), BF16),
            pltpu.VMEM((width, heads), BF16),
            pltpu.VMEM((count, width), BF16),
            pltpu.VMEM((count, heads), BF16),
            dma((2, 4, devices)),
            dma((2, devices)),
            dma((2,)),
        ],
        compiler_params=pltpu.CompilerParams(
            collective_id=0, has_side_effects=True, vmem_limit_bytes=VMEM_BYTES
        ),
    )(
        lengths.reshape(1, 1),
        tokens,
        w_qkv,
        w_out,
        attention_gain.reshape(1, width),
        expert_gain.reshape(1, width),
    )
    slot_ids = slot_numbers(routed_expert, experts, capacity)
    slots = jnp.arange(experts * capacity, dtype=jnp.int32)
    perm = (slots[:, None] == slot_ids[None, :]).astype(BF16)
    perm = perm.reshape(experts, capacity, count)
    perm_t = jnp.swapaxes(perm, 1, 2)
    units = w_gate.shape[1]
    tile = width // TILES
    half_a = capacity * 3 // 5 // 16 * 16
    return pl.pallas_call(
        functools.partial(expert_kernel, half_a),
        out_shape=jax.ShapeDtypeStruct((count, width), BF16),
        in_specs=[vmem] * 4 + [anywhere] * 3,
        out_specs=vmem,
        scratch_shapes=[
            pltpu.VMEM((width, units), BF16),
            pltpu.VMEM((width, units), BF16),
            pltpu.VMEM((units, width), BF16),
            pltpu.VMEM((2, 8, capacity, width), BF16),
            pltpu.VMEM((capacity, width), BF16),
            pltpu.VMEM((8 * capacity, units), BF16),
            pltpu.VMEM((2 * TILES, 8, capacity, tile), BF16),
            pltpu.VMEM((2 * TILES, 4, capacity, tile), BF16),
            pltpu.VMEM((2 * TILES, half_a, tile), BF16),
            pltpu.VMEM((2 * TILES, capacity - half_a, tile), BF16),
            pltpu.VMEM((2 * TILES, capacity, tile), BF16),
            pltpu.VMEM((2 * TILES, capacity, tile), BF16),
            pltpu.VMEM((TILES, capacity, tile), BF16),
            pltpu.VMEM((TILES, capacity, tile), BF16),
            pltpu.VMEM((TILES, capacity, tile), BF16),
            dma((3,)),
            dma((2, 8)),
            dma((2, 8)),
            dma((2,)),
            dma((5, 2 * TILES)),
            dma((5, 2 * TILES)),
            dma((TILES,)),
            dma((TILES,)),
        ],
        compiler_params=pltpu.CompilerParams(
            collective_id=1, has_side_effects=True, vmem_limit_bytes=VMEM_BYTES
        ),
    )(ein, after, perm, perm_t, w_gate, w_up, w_down)


def solution(mesh):
    plane = mesh.shape["tensor"] == 1 and mesh.shape["expert"] == 2 * GROUP
    return jax.shard_map(
        fast_body if plane else body,
        mesh=mesh,
        in_specs=(
            P(("groups", "expert"), None),
            P(("groups", "expert")),
            P(("groups", "expert"), None),
            P(),
            P("expert", "tensor"),
            P("expert", "tensor"),
            P("expert", "tensor"),
            P("expert", "tensor"),
            P(),
            P(None, ("expert", "tensor")),
            P(None, ("expert", "tensor")),
            P(("expert", "tensor"), None),
        ),
        out_specs=P(("groups", "expert"), "tensor"),
        check_vma=False,
    )
```

```python
import functools

import jax
import jax.numpy as jnp
from jax import lax
from jax.experimental import pallas as pl
from jax.experimental.pallas import tpu as pltpu
from jax.sharding import PartitionSpec as P

HEAD = 128
GROUP = 8


def rms_scale(values, gain_vector):
    widened = values.astype(jnp.float32)
    mean_square = jnp.mean(widened * widened, axis=-1, keepdims=True)
    return (widened * lax.rsqrt(mean_square + 1e-05) * gain_vector).astype(jnp.bfloat16)


def slot_numbers(routed, experts, capacity):
    chosen = routed[:, 0]
    one_hot = (chosen[:, None] == jnp.arange(experts, dtype=jnp.int32)[None, :]).astype(jnp.int32)
    running = jnp.cumsum(one_hot, axis=0) - 1
    within = jnp.sum(running * one_hot, axis=1)
    return chosen * capacity + within


def attend(query_rows, key_rows, value_rows, length):
    token_count = query_rows.shape[0]
    head_shape = (token_count, query_rows.shape[1] // HEAD, HEAD)
    scores = jnp.einsum(
        "qhd,khd->hqk",
        query_rows.reshape(head_shape),
        key_rows.reshape(head_shape),
        preferred_element_type=jnp.float32,
    ) * HEAD ** (-0.5)
    positions = jnp.arange(token_count, dtype=jnp.int32)
    allowed = (positions[None, :] <= positions[:, None]) & (positions[None, :] < length)
    scores = jnp.where(allowed[None], scores, -1e30)
    weights = jax.nn.softmax(scores, axis=-1).astype(jnp.bfloat16)
    context = jnp.einsum(
        "hqk,khd->qhd", weights, value_rows.reshape(head_shape), preferred_element_type=jnp.float32
    ).astype(jnp.bfloat16)
    return context.reshape(token_count, -1)


def swiglu_part(arrived_block, gate_weight, up_weight, down_weight):
    gate_sum = jnp.einsum(
        "scd,df->scf", arrived_block, gate_weight, preferred_element_type=jnp.float32
    )
    upward = jnp.einsum("scd,df->scf", arrived_block, up_weight, preferred_element_type=jnp.float32)
    hidden = (jax.nn.silu(gate_sum) * upward).astype(jnp.bfloat16)
    return jnp.einsum("scf,fd->scd", hidden, down_weight, preferred_element_type=jnp.float32)


def body(
    tokens,
    lengths,
    routed_expert,
    attention_gain,
    w_query,
    w_key,
    w_value,
    w_out,
    expert_gain,
    w_gate,
    w_up,
    w_down,
):
    token_count = tokens.shape[0]
    model_width = tokens.shape[1]
    normed = rms_scale(tokens, attention_gain)
    query_sum = jnp.dot(
        normed,
        lax.all_gather(w_query, "expert", axis=0, tiled=True),
        preferred_element_type=jnp.float32,
    )
    key_sum = jnp.dot(
        normed,
        lax.all_gather(w_key, "expert", axis=0, tiled=True),
        preferred_element_type=jnp.float32,
    )
    value_sum = jnp.dot(
        normed,
        lax.all_gather(w_value, "expert", axis=0, tiled=True),
        preferred_element_type=jnp.float32,
    )
    context = attend(
        query_sum.astype(jnp.bfloat16),
        key_sum.astype(jnp.bfloat16),
        value_sum.astype(jnp.bfloat16),
        lengths[0],
    )
    partial_out = lax.dot_general(
        context,
        lax.all_gather(w_out, "expert", axis=0, tiled=True),
        (((1,), (1,)), ((), ())),
        preferred_element_type=jnp.float32,
    )
    cores = lax.axis_size("tensor")
    core_index = lax.axis_index("tensor")
    summed = lax.psum(partial_out, "tensor")
    after_attention = (tokens.astype(jnp.float32) + summed).astype(jnp.bfloat16)
    expert_input = rms_scale(after_attention, expert_gain)
    devices_along = lax.axis_size("expert")
    expert_count = devices_along // GROUP
    capacity = min(token_count, 2 * max(1, 5 * token_count // (8 * expert_count)))
    slot_ids = slot_numbers(routed_expert, expert_count, capacity)
    outgoing_all = (
        jnp.zeros((expert_count * capacity, model_width), jnp.bfloat16)
        .at[slot_ids]
        .set(expert_input)
    )
    outgoing_all = jnp.repeat(
        outgoing_all.reshape(expert_count, capacity, model_width), GROUP, axis=0
    )
    half_width = model_width // cores
    arrived = swiglu_part(
        lax.all_to_all(outgoing_all, "expert", split_axis=0, concat_axis=0, tiled=True),
        w_gate,
        w_up,
        w_down,
    )
    reduced = lax.psum_scatter(arrived, "tensor", scatter_dimension=2, tiled=True).astype(
        jnp.bfloat16
    )
    returned = lax.all_to_all(reduced, "expert", split_axis=0, concat_axis=0, tiled=True)
    part_sums = returned.reshape(expert_count, GROUP, capacity, half_width).astype(jnp.float32)
    expert_rows = jnp.sum(part_sums, axis=1).reshape(expert_count * capacity, half_width)[slot_ids]
    after_half = lax.dynamic_slice_in_dim(after_attention, core_index * half_width, half_width, 1)
    return (after_half.astype(jnp.float32) + expert_rows).astype(jnp.bfloat16)


BF16 = jnp.bfloat16
F32 = jnp.float32
VMEM_BYTES = 60 * 1024 * 1024
TILES = 4


def remote(src, dst, send, recv, target):
    return pltpu.make_async_remote_copy(
        src_ref=src,
        dst_ref=dst,
        send_sem=send,
        recv_sem=recv,
        device_id={"expert": target},
        device_id_type=pl.DeviceIdType.MESH,
    )


def greet(targets):
    barrier = pltpu.get_barrier_semaphore()
    for target in targets:
        pl.semaphore_signal(
            barrier, inc=1, device_id={"expert": target}, device_id_type=pl.DeviceIdType.MESH
        )
    pl.semaphore_wait(barrier, len(targets))


def place():
    me = lax.axis_index("expert")
    core = me % 2
    x = (me // 2) % 2
    z = me // 4
    return me, core, x, z


def gather_kernel(
    lengths,
    tokens,
    w_query,
    w_key,
    w_value,
    w_out,
    gain,
    egain,
    after,
    ein,
    qkv_full,
    out_full,
    normed,
    ctx,
    send,
    recv,
    local,
):
    me, core, x, z = place()
    plane = lax.axis_index("groups")
    shard, heads = w_out.shape
    third = shard // 3
    sib = me + 1 - 2 * core
    across = me + 2 - 4 * x
    fulls = (qkv_full, out_full)

    def rows(who, start, count):
        return pl.ds(pl.multiple_of(who * shard + start, 64), count)

    copies = []
    for k, own in enumerate((w_query, w_key, w_value)):
        into = qkv_full.at[rows(me, 0, shard), pl.ds(k * heads, heads)]
        copies.append(pltpu.make_async_copy(own, into, local.at[k]))
    copies.append(pltpu.make_async_copy(w_out, out_full.at[rows(me, 0, shard)], local.at[3]))
    for copy in copies:
        copy.start()
    barrier = pltpu.get_barrier_semaphore()
    other = {"groups": 1 - plane, "expert": me}
    for target in (sib, across, (me + 4) % 16, (me + 12) % 16):
        pl.semaphore_signal(
            barrier, inc=1, device_id={"expert": target}, device_id_type=pl.DeviceIdType.MESH
        )
    pl.semaphore_signal(barrier, inc=1, device_id=other, device_id_type=pl.DeviceIdType.MESH)
    for copy in copies:
        copy.wait()
    pl.semaphore_wait(barrier, 5)

    targets = (
        {"expert": me + 4},
        {"expert": me - 4},
        {"expert": across},
        {"expert": sib},
        other,
        {"expert": sib},
    )

    def block_of(g, direction, who):
        start, count = third * plane, 2 * third
        if direction == 4:
            start, count = 2 * third * plane, third
        elif direction == 5:
            start, count = 2 * third * (1 - plane), third
        return fulls[g].at[rows(who, start, count)]

    def move(g, direction, who):
        block = block_of(g, direction, who)
        return pltpu.make_async_remote_copy(
            src_ref=block,
            dst_ref=block,
            send_sem=send.at[g, direction, who],
            recv_sem=recv.at[g, direction // 4, who],
            device_id=targets[direction],
            device_id_type=pl.DeviceIdType.MESH,
        )

    def arrived(g, who):
        move(g, 3, who).wait_recv()

    def arrived_third(g, who):
        move(g, 5, who).wait_recv()

    def start(copy):
        copy.start()

    def finish(copy):
        copy.wait_send()

    def each_up(who, act, g):
        @pl.when(z < 3)
        def _():
            act(move(g, 0, who))

    def each_down(who, act, g):
        @pl.when(z > 0)
        def _():
            act(move(g, 1, who))

    def own(g, act):
        each_up(me, act, g)
        each_down(me, act, g)
        act(move(g, 2, me))
        act(move(g, 3, me))
        act(move(g, 5, me))

    def column(g, d, act, wait):
        @pl.when(z >= d)
        def _():
            who = me - 4 * d
            if wait:
                arrived(g, who)
            each_up(who, act, g)
            for direction in (2, 4, 3):
                act(move(g, direction, who))

        @pl.when(z + d <= 3)
        def _():
            who = me + 4 * d
            if wait:
                arrived(g, who)
            each_down(who, act, g)
            for direction in (2, 4, 3):
                act(move(g, direction, who))

    def crossed(g, d, act, wait):
        def pass_on(who):
            if wait:
                arrived(g, who)
            act(move(g, 4, who))
            act(move(g, 3, who))

        if d == 0:
            pass_on(across)
            return

        @pl.when(z >= d)
        def _():
            pass_on(across - 4 * d)

        @pl.when(z + d <= 3)
        def _():
            pass_on(across + 4 * d)

    def thirds(g, d, act, wait):
        def pass_on(who):
            if wait:
                arrived_third(g, who)
            act(move(g, 5, who))

        if d == 0:
            pass_on(across)
            return

        @pl.when(z >= d)
        def _():
            pass_on(me - 4 * d)
            pass_on(across - 4 * d)

        @pl.when(z + d <= 3)
        def _():
            pass_on(me + 4 * d)
            pass_on(across + 4 * d)

    def siblings(g):
        for zz in range(4):
            for xx in range(2):
                arrived(g, (zz * 2 + xx) * 2 + 1 - core)
                arrived_third(g, (zz * 2 + xx) * 2 + 1 - core)

    own(0, start)
    wide = tokens[...].astype(F32)
    mean_square = jnp.mean(wide * wide, axis=-1, keepdims=True)
    normed[...] = (wide * lax.rsqrt(mean_square + 1e-05) * gain[...]).astype(BF16)
    for d in (1, 2, 3):
        column(0, d, start, True)
        crossed(0, d - 1, start, True)
    own(1, start)
    crossed(0, 3, start, True)
    for d in (0, 1, 2, 3):
        thirds(0, d, start, True)
    for d in (1, 2, 3):
        column(1, d, start, True)
        crossed(1, d - 1, start, True)
    siblings(0)

    width = qkv_full.shape[1] // 3
    qkv = jnp.dot(normed[...], qkv_full[...], preferred_element_type=F32).astype(BF16)
    count = tokens.shape[0]
    qpos = lax.broadcasted_iota(jnp.int32, (count, count), 0)
    kpos = lax.broadcasted_iota(jnp.int32, (count, count), 1)
    allowed = (kpos <= qpos) & (kpos < lengths[...])
    for head in range(width // HEAD):
        at = head * HEAD
        query = qkv[:, at : at + HEAD]
        key = qkv[:, width + at : width + at + HEAD]
        value = qkv[:, 2 * width + at : 2 * width + at + HEAD]
        scores = lax.dot_general(
            query, key, (((1,), (1,)), ((), ())), preferred_element_type=F32
        ) * HEAD ** (-0.5)
        scores = jnp.where(allowed, scores, -1e30)
        peak = jnp.max(scores, axis=-1, keepdims=True)
        weights = jnp.exp(scores - peak)
        weights = (weights / jnp.sum(weights, axis=-1, keepdims=True)).astype(BF16)
        ctx[:, at : at + HEAD] = jnp.dot(weights, value, preferred_element_type=F32).astype(BF16)
    crossed(1, 3, start, True)
    for d in (0, 1, 2, 3):
        thirds(1, d, start, True)
    siblings(1)
    attended = lax.dot_general(
        ctx[...], out_full[...], (((1,), (1,)), ((), ())), preferred_element_type=F32
    )
    after[...] = (tokens[...].astype(F32) + attended).astype(BF16)
    wide = after[...].astype(F32)
    mean_square = jnp.mean(wide * wide, axis=-1, keepdims=True)
    ein[...] = (wide * lax.rsqrt(mean_square + 1e-05) * egain[...]).astype(BF16)
    for g in (0, 1):
        own(g, finish)
        for d in (0, 1, 2, 3):
            if d:
                column(g, d, finish, False)
            crossed(g, d, finish, False)
            thirds(g, d, finish, False)


def expert_kernel(
    half_a,
    ein,
    after,
    routed,
    w_gate,
    w_up,
    w_down,
    out,
    gate_v,
    up_v,
    down_v,
    rows_in,
    far_own,
    hidden,
    part,
    from_sib,
    diag_x,
    diag_z,
    sum_x,
    sum_z,
    near_sum,
    far_sum,
    far_back,
    wsem,
    gsend,
    grecv,
    csem,
    rsend,
    rrecv,
    fsend,
    frecv,
):
    me, core, x, z = place()
    near = z // 2
    sib = me + 1 - 2 * core
    across = me + 2 - 4 * x
    along = me + 4 - 8 * (z % 2)
    mirror = me + 8 - 16 * near
    slots, cap, width = rows_in.shape[1], rows_in.shape[2], rows_in.shape[3]
    loads = []
    for k, (src, dst) in enumerate(((w_gate, gate_v), (w_up, up_v), (w_down, down_v))):
        copy = pltpu.make_async_copy(src, dst, wsem.at[k])
        copy.start()
        loads.append(copy)
    count = ein.shape[0]
    chosen = routed[...]
    earlier = lax.broadcasted_iota(jnp.int32, (count, count), 0) <= lax.broadcasted_iota(
        jnp.int32, (count, count), 1
    )

    def slot_matrix(expert):
        named = jnp.broadcast_to(chosen == expert, (16, count))
        number = jnp.dot(
            named.astype(BF16), earlier.astype(BF16), preferred_element_type=F32
        ).astype(jnp.int32)[0:1]
        slot = lax.broadcasted_iota(jnp.int32, (cap, count), 0) + 1
        return ((slot == number) & (chosen == expert)).astype(BF16)

    far_pick = slot_matrix(1 - near)
    near_pick = slot_matrix(near)
    far_own[...] = jnp.dot(far_pick, ein[...], preferred_element_type=F32).astype(BF16)
    rows_in[0, 0] = jnp.dot(near_pick, ein[...], preferred_element_type=F32).astype(BF16)
    greet((sib, across, along, mirror))

    started = []

    def go(copy):
        copy.start()
        started.append(copy)
        return copy

    def gather_own(k):
        own = rows_in.at[k, 0]
        to_x = go(remote(own, rows_in.at[k, 1], gsend.at[k, 0], grecv.at[k, 0], across))
        to_z = go(remote(own, rows_in.at[k, 2], gsend.at[k, 1], grecv.at[k, 1], along))
        to_s = go(remote(own, rows_in.at[k, 4], gsend.at[k, 2], grecv.at[k, 2], sib))
        return to_x, to_z, to_s

    def gather_pass(k, first):
        first[0].wait_recv()
        from_x = rows_in.at[k, 1]
        rest = cap - half_a
        d_z = go(
            remote(
                from_x.at[pl.ds(half_a, rest)],
                rows_in.at[k, 3, pl.ds(half_a, rest)],
                gsend.at[k, 3],
                grecv.at[k, 3],
                along,
            )
        )
        s1 = go(remote(from_x, rows_in.at[k, 5], gsend.at[k, 4], grecv.at[k, 4], sib))
        first[1].wait_recv()
        from_z = rows_in.at[k, 2]
        d_x = go(
            remote(
                from_z.at[pl.ds(0, half_a)],
                rows_in.at[k, 3, pl.ds(0, half_a)],
                gsend.at[k, 5],
                grecv.at[k, 5],
                across,
            )
        )
        s2 = go(remote(from_z, rows_in.at[k, 6], gsend.at[k, 6], grecv.at[k, 6], sib))
        return d_z, d_x, s1, s2

    def gather_last(k, second):
        second[0].wait_recv()
        second[1].wait_recv()
        return go(
            remote(rows_in.at[k, 3], rows_in.at[k, 7], gsend.at[k, 7], grecv.at[k, 7], sib)
        )

    def gather_done(first, second, third):
        first[2].wait_recv()
        second[2].wait_recv()
        second[3].wait_recv()
        third.wait_recv()

    fan = gate_v.shape[1] // TILES
    tile = width // TILES

    def up_tile(k, t):
        cols = pl.ds(pl.multiple_of(t * fan, fan), fan)
        given = rows_in[k].reshape(slots * cap, width)
        gate = jnp.dot(given, gate_v[:, cols], preferred_element_type=F32)
        upward = jnp.dot(given, up_v[:, cols], preferred_element_type=F32)
        hidden[:, cols] = (jax.nn.silu(gate) * upward).astype(BF16)

    def down_tile(k, t):
        cols = pl.ds(pl.multiple_of(t * tile, tile), tile)
        total = jnp.dot(hidden[...], down_v[:, cols], preferred_element_type=F32)
        part[k * TILES + t] = total.astype(BF16).reshape(slots, cap, tile)

    def summing(kind, i):
        rest = cap - half_a
        ends = (
            (part.at[i, pl.ds(4, 4)], from_sib.at[i], sib),
            (part.at[i, 3, pl.ds(0, half_a)], diag_x.at[i], across),
            (part.at[i, 3, pl.ds(half_a, rest)], diag_z.at[i], along),
            (part.at[i, 1], sum_x.at[i], across),
            (part.at[i, 2], sum_z.at[i], along),
        )[kind]
        return remote(ends[0], ends[1], rsend.at[kind, i], rrecv.at[kind, i], ends[2])

    def plus(a, b):
        return (a.astype(F32) + b.astype(F32)).astype(BF16)

    def step_core(i):
        summing(0, i).wait_recv()
        part[i, 3] = plus(part[i, 3], from_sib[i, 3])
        summing(1, i).start()
        summing(2, i).start()
        part[i, 0:3] = plus(part[i, 0:3], from_sib[i, 0:3])

    def step_diag(i):
        summing(1, i).wait_recv()
        part[i, 2, 0:half_a] = plus(part[i, 2, 0:half_a], diag_x[i])
        summing(4, i).start()
        summing(2, i).wait_recv()
        part[i, 1, half_a:cap] = plus(part[i, 1, half_a:cap], diag_z[i])
        summing(3, i).start()

    def total_of(i):
        summing(3, i).wait_recv()
        summing(4, i).wait_recv()
        total = part[i, 0].astype(F32) + sum_x[i].astype(F32) + sum_z[i].astype(F32)
        return total.astype(BF16)

    def returning(t):
        return remote(far_sum.at[t], far_back.at[t], fsend.at[t], frecv.at[t], mirror)

    def loop(body):
        lax.fori_loop(0, TILES, lambda t, c: (body(t), c)[1], 0)

    near_first = gather_own(0)
    crossing = go(remote(far_own, rows_in.at[1, 0], csem.at[0], csem.at[1], mirror))
    near_second = gather_pass(0, near_first)
    near_third = gather_last(0, near_second)
    crossing.wait_recv()
    far_first = gather_own(1)
    gather_done(near_first, near_second, near_third)
    for copy in loads:
        copy.wait()
    loop(functools.partial(up_tile, 0))
    far_second = gather_pass(1, far_first)

    def near_down(t):
        down_tile(0, t)
        summing(0, t).start()

        @pl.when(t > 0)
        def _():
            step_core(t - 1)

    loop(near_down)
    step_core(TILES - 1)
    far_third = gather_last(1, far_second)
    gather_done(far_first, far_second, far_third)

    def far_up(t):
        up_tile(1, t)
        step_diag(t)

    loop(far_up)

    def far_down(t):
        i = TILES + t
        down_tile(1, t)
        summing(0, i).start()

        @pl.when(t > 0)
        def _():
            step_core(i - 1)

        near_sum[t] = total_of(t)

    loop(far_down)
    step_core(2 * TILES - 1)
    loop(lambda t: step_diag(TILES + t))

    def far_total(t):
        far_sum[t] = total_of(TILES + t)
        returning(t).start()

    loop(far_total)

    def finish(t):
        cols = pl.ds(pl.multiple_of(t * tile, tile), tile)
        returning(t).wait_recv()
        first = (((0,), (0,)), ((), ()))
        moved = lax.dot_general(near_pick, near_sum[t], first, preferred_element_type=F32)
        moved = moved + lax.dot_general(far_pick, far_back[t], first, preferred_element_type=F32)
        out[:, cols] = (after[:, cols].astype(F32) + moved).astype(BF16)
        returning(t).wait_send()

    loop(finish)
    for copy in started:
        copy.wait_send()

    def drain(i, c):
        for kind in range(5):
            summing(kind, i).wait_send()
        return c

    lax.fori_loop(0, 2 * TILES, drain, 0)


def fast_body(
    tokens,
    lengths,
    routed_expert,
    attention_gain,
    w_query,
    w_key,
    w_value,
    w_out,
    expert_gain,
    w_gate,
    w_up,
    w_down,
):
    count, width = tokens.shape
    devices = lax.axis_size("expert")
    experts = devices // GROUP
    capacity = min(count, 2 * max(1, 5 * count // (8 * experts)))
    vmem = pl.BlockSpec(memory_space=pltpu.VMEM)
    anywhere = pl.BlockSpec(memory_space=pl.ANY)
    heads = w_query.shape[1]
    dma = pltpu.SemaphoreType.DMA
    after, ein = pl.pallas_call(
        gather_kernel,
        out_shape=[jax.ShapeDtypeStruct((count, width), BF16)] * 2,
        in_specs=[vmem] * 2 + [anywhere] * 4 + [vmem] * 2,
        out_specs=[vmem] * 2,
        scratch_shapes=[
            pltpu.VMEM((width, 3 * heads), BF16),
            pltpu.VMEM((width, heads), BF16),
            pltpu.VMEM((count, width), BF16),
            pltpu.VMEM((count, heads), BF16),
            dma((2, 6, devices)),
            dma((2, 2, devices)),
            dma((4,)),
        ],
        compiler_params=pltpu.CompilerParams(
            collective_id=0, has_side_effects=True, vmem_limit_bytes=VMEM_BYTES
        ),
    )(
        lengths.reshape(1, 1),
        tokens,
        w_query,
        w_key,
        w_value,
        w_out,
        attention_gain.reshape(1, width),
        expert_gain.reshape(1, width),
    )
    units = w_gate.shape[1]
    tile = width // TILES
    half_a = capacity * 3 // 5 // 16 * 16
    return pl.pallas_call(
        functools.partial(expert_kernel, half_a),
        out_shape=jax.ShapeDtypeStruct((count, width), BF16),
        in_specs=[vmem] * 3 + [anywhere] * 3,
        out_specs=vmem,
        scratch_shapes=[
            pltpu.VMEM((width, units), BF16),
            pltpu.VMEM((width, units), BF16),
            pltpu.VMEM((units, width), BF16),
            pltpu.VMEM((2, 8, capacity, width), BF16),
            pltpu.VMEM((capacity, width), BF16),
            pltpu.VMEM((8 * capacity, units), BF16),
            pltpu.VMEM((2 * TILES, 8, capacity, tile), BF16),
            pltpu.VMEM((2 * TILES, 4, capacity, tile), BF16),
            pltpu.VMEM((2 * TILES, half_a, tile), BF16),
            pltpu.VMEM((2 * TILES, capacity - half_a, tile), BF16),
            pltpu.VMEM((2 * TILES, capacity, tile), BF16),
            pltpu.VMEM((2 * TILES, capacity, tile), BF16),
            pltpu.VMEM((TILES, capacity, tile), BF16),
            pltpu.VMEM((TILES, capacity, tile), BF16),
            pltpu.VMEM((TILES, capacity, tile), BF16),
            dma((3,)),
            dma((2, 8)),
            dma((2, 8)),
            dma((2,)),
            dma((5, 2 * TILES)),
            dma((5, 2 * TILES)),
            dma((TILES,)),
            dma((TILES,)),
        ],
        compiler_params=pltpu.CompilerParams(
            collective_id=1, has_side_effects=True, vmem_limit_bytes=VMEM_BYTES
        ),
    )(ein, after, routed_expert.reshape(1, count), w_gate, w_up, w_down)


def solution(mesh):
    plane = mesh.shape["tensor"] == 1 and mesh.shape["expert"] == 2 * GROUP
    plane = plane and mesh.shape["groups"] == 2
    return jax.shard_map(
        fast_body if plane else body,
        mesh=mesh,
        in_specs=(
            P(("groups", "expert"), None),
            P(("groups", "expert")),
            P(("groups", "expert"), None),
            P(),
            P("expert", "tensor"),
            P("expert", "tensor"),
            P("expert", "tensor"),
            P("expert", "tensor"),
            P(),
            P(None, ("expert", "tensor")),
            P(None, ("expert", "tensor")),
            P(("expert", "tensor"), None),
        ),
        out_specs=P(("groups", "expert"), "tensor"),
        check_vma=False,
    )
```

```python
import functools

import jax
import jax.numpy as jnp
from jax import lax
from jax.experimental import pallas as pl
from jax.experimental.pallas import tpu as pltpu
from jax.sharding import PartitionSpec as P

HEAD = 128
GROUP = 8


def rms_scale(values, gain_vector):
    widened = values.astype(jnp.float32)
    mean_square = jnp.mean(widened * widened, axis=-1, keepdims=True)
    return (widened * lax.rsqrt(mean_square + 1e-05) * gain_vector).astype(jnp.bfloat16)


def slot_numbers(routed, experts, capacity):
    chosen = routed[:, 0]
    one_hot = (chosen[:, None] == jnp.arange(experts, dtype=jnp.int32)[None, :]).astype(jnp.int32)
    running = jnp.cumsum(one_hot, axis=0) - 1
    within = jnp.sum(running * one_hot, axis=1)
    return chosen * capacity + within


def attend(query_rows, key_rows, value_rows, length):
    token_count = query_rows.shape[0]
    head_shape = (token_count, query_rows.shape[1] // HEAD, HEAD)
    scores = jnp.einsum(
        "qhd,khd->hqk",
        query_rows.reshape(head_shape),
        key_rows.reshape(head_shape),
        preferred_element_type=jnp.float32,
    ) * HEAD ** (-0.5)
    positions = jnp.arange(token_count, dtype=jnp.int32)
    allowed = (positions[None, :] <= positions[:, None]) & (positions[None, :] < length)
    scores = jnp.where(allowed[None], scores, -1e30)
    weights = jax.nn.softmax(scores, axis=-1).astype(jnp.bfloat16)
    context = jnp.einsum(
        "hqk,khd->qhd", weights, value_rows.reshape(head_shape), preferred_element_type=jnp.float32
    ).astype(jnp.bfloat16)
    return context.reshape(token_count, -1)


def swiglu_part(arrived_block, gate_weight, up_weight, down_weight):
    gate_sum = jnp.einsum(
        "scd,df->scf", arrived_block, gate_weight, preferred_element_type=jnp.float32
    )
    upward = jnp.einsum("scd,df->scf", arrived_block, up_weight, preferred_element_type=jnp.float32)
    hidden = (jax.nn.silu(gate_sum) * upward).astype(jnp.bfloat16)
    return jnp.einsum("scf,fd->scd", hidden, down_weight, preferred_element_type=jnp.float32)


def body(
    tokens,
    lengths,
    routed_expert,
    attention_gain,
    w_query,
    w_key,
    w_value,
    w_out,
    expert_gain,
    w_gate,
    w_up,
    w_down,
):
    token_count = tokens.shape[0]
    model_width = tokens.shape[1]
    normed = rms_scale(tokens, attention_gain)
    query_sum = jnp.dot(
        normed,
        lax.all_gather(w_query, "expert", axis=0, tiled=True),
        preferred_element_type=jnp.float32,
    )
    key_sum = jnp.dot(
        normed,
        lax.all_gather(w_key, "expert", axis=0, tiled=True),
        preferred_element_type=jnp.float32,
    )
    value_sum = jnp.dot(
        normed,
        lax.all_gather(w_value, "expert", axis=0, tiled=True),
        preferred_element_type=jnp.float32,
    )
    context = attend(
        query_sum.astype(jnp.bfloat16),
        key_sum.astype(jnp.bfloat16),
        value_sum.astype(jnp.bfloat16),
        lengths[0],
    )
    partial_out = lax.dot_general(
        context,
        lax.all_gather(w_out, "expert", axis=0, tiled=True),
        (((1,), (1,)), ((), ())),
        preferred_element_type=jnp.float32,
    )
    cores = lax.axis_size("tensor")
    core_index = lax.axis_index("tensor")
    summed = lax.psum(partial_out, "tensor")
    after_attention = (tokens.astype(jnp.float32) + summed).astype(jnp.bfloat16)
    expert_input = rms_scale(after_attention, expert_gain)
    devices_along = lax.axis_size("expert")
    expert_count = devices_along // GROUP
    capacity = min(token_count, 2 * max(1, 5 * token_count // (8 * expert_count)))
    slot_ids = slot_numbers(routed_expert, expert_count, capacity)
    outgoing_all = (
        jnp.zeros((expert_count * capacity, model_width), jnp.bfloat16)
        .at[slot_ids]
        .set(expert_input)
    )
    outgoing_all = jnp.repeat(
        outgoing_all.reshape(expert_count, capacity, model_width), GROUP, axis=0
    )
    half_width = model_width // cores
    arrived = swiglu_part(
        lax.all_to_all(outgoing_all, "expert", split_axis=0, concat_axis=0, tiled=True),
        w_gate,
        w_up,
        w_down,
    )
    reduced = lax.psum_scatter(arrived, "tensor", scatter_dimension=2, tiled=True).astype(
        jnp.bfloat16
    )
    returned = lax.all_to_all(reduced, "expert", split_axis=0, concat_axis=0, tiled=True)
    part_sums = returned.reshape(expert_count, GROUP, capacity, half_width).astype(jnp.float32)
    expert_rows = jnp.sum(part_sums, axis=1).reshape(expert_count * capacity, half_width)[slot_ids]
    after_half = lax.dynamic_slice_in_dim(after_attention, core_index * half_width, half_width, 1)
    return (after_half.astype(jnp.float32) + expert_rows).astype(jnp.bfloat16)


BF16 = jnp.bfloat16
F32 = jnp.float32
VMEM_BYTES = 60 * 1024 * 1024
TILES = 4


def remote(src, dst, send, recv, target):
    return pltpu.make_async_remote_copy(
        src_ref=src,
        dst_ref=dst,
        send_sem=send,
        recv_sem=recv,
        device_id={"expert": target},
        device_id_type=pl.DeviceIdType.MESH,
    )


def greet(targets):
    barrier = pltpu.get_barrier_semaphore()
    for target in targets:
        pl.semaphore_signal(
            barrier, inc=1, device_id={"expert": target}, device_id_type=pl.DeviceIdType.MESH
        )
    pl.semaphore_wait(barrier, len(targets))


def place():
    me = lax.axis_index("expert")
    core = me % 2
    x = (me // 2) % 2
    z = me // 4
    return me, core, x, z


def gather_kernel(
    lengths,
    tokens,
    w_query,
    w_key,
    w_value,
    w_out,
    gain,
    egain,
    after,
    ein,
    qkv_full,
    out_full,
    normed,
    ctx,
    send,
    recv,
    local,
):
    me, core, x, z = place()
    plane = lax.axis_index("groups")
    shard, heads = w_out.shape
    third = shard // 3
    sib = me + 1 - 2 * core
    across = me + 2 - 4 * x
    fulls = (qkv_full, out_full)

    def rows(who, start, count):
        return pl.ds(pl.multiple_of(who * shard + start, 64), count)

    copies = []
    for k, own in enumerate((w_query, w_key, w_value)):
        into = qkv_full.at[rows(me, 0, shard), pl.ds(k * heads, heads)]
        copies.append(pltpu.make_async_copy(own, into, local.at[k]))
    copies.append(pltpu.make_async_copy(w_out, out_full.at[rows(me, 0, shard)], local.at[3]))
    for copy in copies:
        copy.start()
    barrier = pltpu.get_barrier_semaphore()
    other = {"groups": 1 - plane, "expert": me}
    for target in (sib, across, (me + 4) % 16, (me + 12) % 16):
        pl.semaphore_signal(
            barrier, inc=1, device_id={"expert": target}, device_id_type=pl.DeviceIdType.MESH
        )
    pl.semaphore_signal(barrier, inc=1, device_id=other, device_id_type=pl.DeviceIdType.MESH)
    for copy in copies:
        copy.wait()
    pl.semaphore_wait(barrier, 5)

    targets = (
        {"expert": me + 4},
        {"expert": me - 4},
        {"expert": across},
        {"expert": sib},
        other,
        {"expert": sib},
    )

    def block_of(g, direction, who):
        start, count = third * plane, 2 * third
        if direction == 4:
            start, count = 2 * third * plane, third
        elif direction == 5:
            start, count = 2 * third * (1 - plane), third
        return fulls[g].at[rows(who, start, count)]

    def move(g, direction, who):
        block = block_of(g, direction, who)
        return pltpu.make_async_remote_copy(
            src_ref=block,
            dst_ref=block,
            send_sem=send.at[g, direction, who],
            recv_sem=recv.at[g, direction // 4, who],
            device_id=targets[direction],
            device_id_type=pl.DeviceIdType.MESH,
        )

    def arrived(g, who):
        move(g, 3, who).wait_recv()

    def arrived_third(g, who):
        move(g, 5, who).wait_recv()

    def start(copy):
        copy.start()

    def finish(copy):
        copy.wait_send()

    def each_up(who, act, g):
        @pl.when(z < 3)
        def _():
            act(move(g, 0, who))

    def each_down(who, act, g):
        @pl.when(z > 0)
        def _():
            act(move(g, 1, who))

    def own(g, act):
        each_up(me, act, g)
        each_down(me, act, g)
        act(move(g, 2, me))
        act(move(g, 3, me))
        act(move(g, 5, me))

    def column(g, d, act, wait):
        @pl.when(z >= d)
        def _():
            who = me - 4 * d
            if wait:
                arrived(g, who)
            each_up(who, act, g)
            for direction in (2, 4, 3):
                act(move(g, direction, who))

        @pl.when(z + d <= 3)
        def _():
            who = me + 4 * d
            if wait:
                arrived(g, who)
            each_down(who, act, g)
            for direction in (2, 4, 3):
                act(move(g, direction, who))

    def crossed(g, d, act, wait):
        def pass_on(who):
            if wait:
                arrived(g, who)
            act(move(g, 4, who))
            act(move(g, 3, who))

        if d == 0:
            pass_on(across)
            return

        @pl.when(z >= d)
        def _():
            pass_on(across - 4 * d)

        @pl.when(z + d <= 3)
        def _():
            pass_on(across + 4 * d)

    def thirds(g, d, act, wait):
        def pass_on(who):
            if wait:
                arrived_third(g, who)
            act(move(g, 5, who))

        if d == 0:
            pass_on(across)
            return

        @pl.when(z >= d)
        def _():
            pass_on(me - 4 * d)
            pass_on(across - 4 * d)

        @pl.when(z + d <= 3)
        def _():
            pass_on(me + 4 * d)
            pass_on(across + 4 * d)

    def siblings(g):
        for zz in range(4):
            for xx in range(2):
                arrived(g, (zz * 2 + xx) * 2 + 1 - core)
                arrived_third(g, (zz * 2 + xx) * 2 + 1 - core)

    own(0, start)
    wide = tokens[...].astype(F32)
    mean_square = jnp.mean(wide * wide, axis=-1, keepdims=True)
    normed[...] = (wide * lax.rsqrt(mean_square + 1e-05) * gain[...]).astype(BF16)
    for d in (1, 2, 3):
        column(0, d, start, True)
        crossed(0, d - 1, start, True)
    own(1, start)
    crossed(0, 3, start, True)
    for d in (0, 1, 2, 3):
        thirds(0, d, start, True)
    for d in (1, 2, 3):
        column(1, d, start, True)
        crossed(1, d - 1, start, True)
    siblings(0)

    width = qkv_full.shape[1] // 3
    qkv = jnp.dot(normed[...], qkv_full[...], preferred_element_type=F32).astype(BF16)
    count = tokens.shape[0]
    qpos = lax.broadcasted_iota(jnp.int32, (count, count), 0)
    kpos = lax.broadcasted_iota(jnp.int32, (count, count), 1)
    allowed = (kpos <= qpos) & (kpos < lengths[...])
    for head in range(width // HEAD):
        at = head * HEAD
        query = qkv[:, at : at + HEAD]
        key = qkv[:, width + at : width + at + HEAD]
        value = qkv[:, 2 * width + at : 2 * width + at + HEAD]
        scores = lax.dot_general(
            query, key, (((1,), (1,)), ((), ())), preferred_element_type=F32
        ) * HEAD ** (-0.5)
        scores = jnp.where(allowed, scores, -1e30)
        peak = jnp.max(scores, axis=-1, keepdims=True)
        weights = jnp.exp(scores - peak)
        weights = (weights / jnp.sum(weights, axis=-1, keepdims=True)).astype(BF16)
        ctx[:, at : at + HEAD] = jnp.dot(weights, value, preferred_element_type=F32).astype(BF16)
    crossed(1, 3, start, True)
    for d in (0, 1, 2, 3):
        thirds(1, d, start, True)
    siblings(1)
    attended = lax.dot_general(
        ctx[...], out_full[...], (((1,), (1,)), ((), ())), preferred_element_type=F32
    )
    after[...] = (tokens[...].astype(F32) + attended).astype(BF16)
    wide = after[...].astype(F32)
    mean_square = jnp.mean(wide * wide, axis=-1, keepdims=True)
    ein[...] = (wide * lax.rsqrt(mean_square + 1e-05) * egain[...]).astype(BF16)
    for g in (0, 1):
        own(g, finish)
        for d in (0, 1, 2, 3):
            if d:
                column(g, d, finish, False)
            crossed(g, d, finish, False)
            thirds(g, d, finish, False)


def expert_kernel(
    half_a,
    ein,
    after,
    routed,
    w_gate,
    w_up,
    w_down,
    out,
    gate_v,
    up_v,
    down_v,
    rows_in,
    far_own,
    hidden,
    part,
    from_sib,
    diag_x,
    diag_z,
    sum_x,
    sum_z,
    near_sum,
    far_sum,
    far_back,
    wsem,
    gsend,
    grecv,
    csem,
    rsend,
    rrecv,
    fsend,
    frecv,
):
    me, core, x, z = place()
    near = z // 2
    sib = me + 1 - 2 * core
    across = me + 2 - 4 * x
    along = me + 4 - 8 * (z % 2)
    mirror = me + 8 - 16 * near
    slots, cap, width = rows_in.shape[1], rows_in.shape[2], rows_in.shape[3]
    loads = []
    for k, (src, dst) in enumerate(((w_gate, gate_v), (w_up, up_v), (w_down, down_v))):
        copy = pltpu.make_async_copy(src, dst, wsem.at[k])
        copy.start()
        loads.append(copy)
    count = ein.shape[0]
    chosen = routed[...]
    earlier = lax.broadcasted_iota(jnp.int32, (count, count), 0) <= lax.broadcasted_iota(
        jnp.int32, (count, count), 1
    )

    def slot_matrix(expert):
        named = jnp.broadcast_to(chosen == expert, (16, count))
        number = jnp.dot(
            named.astype(BF16), earlier.astype(BF16), preferred_element_type=F32
        ).astype(jnp.int32)[0:1]
        slot = lax.broadcasted_iota(jnp.int32, (cap, count), 0) + 1
        return ((slot == number) & (chosen == expert)).astype(BF16)

    far_pick = slot_matrix(1 - near)
    near_pick = slot_matrix(near)
    far_own[...] = jnp.dot(far_pick, ein[...], preferred_element_type=F32).astype(BF16)
    rows_in[0, 0] = jnp.dot(near_pick, ein[...], preferred_element_type=F32).astype(BF16)
    greet((sib, across, along, mirror))

    fan = gate_v.shape[1] // TILES
    tile = width // TILES

    def columns(t):
        return pl.ds(pl.multiple_of(t * tile, tile), tile)

    def gathering(kind, k, t):
        cut = (half_a + 16, half_a)[k]
        every, lower, upper = pl.ds(0, cap), pl.ds(0, cut), pl.ds(cut, cap - cut)
        source, slot, rows, target = (
            (0, 1, every, across),
            (0, 2, every, along),
            (0, 4, every, sib),
            (1, 3, upper, along),
            (1, 5, every, sib),
            (2, 3, lower, across),
            (2, 6, every, sib),
            (3, 7, every, sib),
        )[kind]
        return remote(
            rows_in.at[k, source, rows, columns(t)],
            rows_in.at[k, slot, rows, columns(t)],
            gsend.at[k, kind, t],
            grecv.at[k, kind, t],
            target,
        )

    def crossing(t):
        return remote(
            far_own.at[:, columns(t)],
            rows_in.at[1, 0, :, columns(t)],
            csem.at[0, t],
            csem.at[1, t],
            mirror,
        )

    def gather_own(k, t):
        for kind in (0, 1, 2):
            gathering(kind, k, t).start()

    def gather_pass(k, t):
        gathering(0, k, t).wait_recv()
        gathering(3, k, t).start()
        gathering(4, k, t).start()
        gathering(1, k, t).wait_recv()
        gathering(5, k, t).start()
        gathering(6, k, t).start()

    def gather_last(k, t):
        gathering(3, k, t).wait_recv()
        gathering(5, k, t).wait_recv()
        gathering(7, k, t).start()

    def gather_done(k, t):
        for kind in (2, 4, 6, 7):
            gathering(kind, k, t).wait_recv()

    def up_tile(k, t):
        cols = pl.ds(pl.multiple_of(t * fan, fan), fan)
        given = rows_in[k].reshape(slots * cap, width)
        gate = jnp.dot(given, gate_v[:, cols], preferred_element_type=F32)
        upward = jnp.dot(given, up_v[:, cols], preferred_element_type=F32)
        hidden[:, cols] = (jax.nn.silu(gate) * upward).astype(BF16)

    def down_tile(k, t):
        cols = columns(t)
        total = jnp.dot(hidden[...], down_v[:, cols], preferred_element_type=F32)
        part[k * TILES + t] = total.astype(BF16).reshape(slots, cap, tile)

    def summing(kind, i):
        rest = cap - half_a
        ends = (
            (part.at[i, pl.ds(4, 4)], from_sib.at[i], sib),
            (part.at[i, 3, pl.ds(0, half_a)], diag_x.at[i], across),
            (part.at[i, 3, pl.ds(half_a, rest)], diag_z.at[i], along),
            (part.at[i, 1], sum_x.at[i], across),
            (part.at[i, 2], sum_z.at[i], along),
        )[kind]
        return remote(ends[0], ends[1], rsend.at[kind, i], rrecv.at[kind, i], ends[2])

    def plus(a, b):
        return (a.astype(F32) + b.astype(F32)).astype(BF16)

    def step_core(i):
        summing(0, i).wait_recv()
        part[i, 3] = plus(part[i, 3], from_sib[i, 3])
        summing(1, i).start()
        summing(2, i).start()
        part[i, 0:3] = plus(part[i, 0:3], from_sib[i, 0:3])

    def step_diag(i):
        summing(1, i).wait_recv()
        part[i, 2, 0:half_a] = plus(part[i, 2, 0:half_a], diag_x[i])
        summing(4, i).start()
        summing(2, i).wait_recv()
        part[i, 1, half_a:cap] = plus(part[i, 1, half_a:cap], diag_z[i])
        summing(3, i).start()

    def total_of(i):
        summing(3, i).wait_recv()
        summing(4, i).wait_recv()
        total = part[i, 0].astype(F32) + sum_x[i].astype(F32) + sum_z[i].astype(F32)
        return total.astype(BF16)

    def returning(t):
        return remote(far_sum.at[t], far_back.at[t], fsend.at[t], frecv.at[t], mirror)

    def loop(body):
        lax.fori_loop(0, TILES, lambda t, c: (body(t), c)[1], 0)

    def begin(t):
        gather_own(0, t)
        crossing(t).start()

    def second(t):
        gather_pass(0, t)
        crossing(t).wait_recv()
        gather_own(1, t)

    loop(begin)
    loop(second)
    loop(functools.partial(gather_last, 0))
    loop(functools.partial(gather_done, 0))
    for copy in loads:
        copy.wait()

    def near_up(t):
        up_tile(0, t)
        gather_pass(1, t)

    loop(near_up)

    def near_down(t):
        down_tile(0, t)
        summing(0, t).start()
        gather_last(1, t)

        @pl.when(t > 0)
        def _():
            step_core(t - 1)

    loop(near_down)
    step_core(TILES - 1)
    loop(functools.partial(gather_done, 1))

    def far_up(t):
        up_tile(1, t)
        step_diag(t)

    loop(far_up)

    def far_steps(t, c):
        i = TILES + t

        @pl.when(t < TILES)
        def _():
            down_tile(1, t)
            summing(0, i).start()
            near_sum[t] = total_of(t)

        @pl.when((t >= 1) & (t < TILES + 1))
        def _():
            step_core(i - 1)

        @pl.when((t >= 2) & (t < TILES + 2))
        def _():
            step_diag(i - 2)

        @pl.when(t >= 3)
        def _():
            far_sum[t - 3] = total_of(i - 3)
            returning(t - 3).start()

        return c

    lax.fori_loop(0, TILES + 3, far_steps, 0)

    def finish(t):
        cols = columns(t)
        returning(t).wait_recv()
        first = (((0,), (0,)), ((), ()))
        moved = lax.dot_general(near_pick, near_sum[t], first, preferred_element_type=F32)
        moved = moved + lax.dot_general(far_pick, far_back[t], first, preferred_element_type=F32)
        out[:, cols] = (after[:, cols].astype(F32) + moved).astype(BF16)

    loop(finish)

    def drain_gather(t):
        returning(t).wait_send()
        crossing(t).wait_send()
        for k in range(2):
            for kind in range(8):
                gathering(kind, k, t).wait_send()

    loop(drain_gather)

    def drain(i, c):
        for kind in range(5):
            summing(kind, i).wait_send()
        return c

    lax.fori_loop(0, 2 * TILES, drain, 0)


def fast_body(
    tokens,
    lengths,
    routed_expert,
    attention_gain,
    w_query,
    w_key,
    w_value,
    w_out,
    expert_gain,
    w_gate,
    w_up,
    w_down,
):
    count, width = tokens.shape
    devices = lax.axis_size("expert")
    experts = devices // GROUP
    capacity = min(count, 2 * max(1, 5 * count // (8 * experts)))
    vmem = pl.BlockSpec(memory_space=pltpu.VMEM)
    anywhere = pl.BlockSpec(memory_space=pl.ANY)
    heads = w_query.shape[1]
    dma = pltpu.SemaphoreType.DMA
    after, ein = pl.pallas_call(
        gather_kernel,
        out_shape=[jax.ShapeDtypeStruct((count, width), BF16)] * 2,
        in_specs=[vmem] * 2 + [anywhere] * 4 + [vmem] * 2,
        out_specs=[vmem] * 2,
        scratch_shapes=[
            pltpu.VMEM((width, 3 * heads), BF16),
            pltpu.VMEM((width, heads), BF16),
            pltpu.VMEM((count, width), BF16),
            pltpu.VMEM((count, heads), BF16),
            dma((2, 6, devices)),
            dma((2, 2, devices)),
            dma((4,)),
        ],
        compiler_params=pltpu.CompilerParams(
            collective_id=0, has_side_effects=True, vmem_limit_bytes=VMEM_BYTES
        ),
    )(
        lengths.reshape(1, 1),
        tokens,
        w_query,
        w_key,
        w_value,
        w_out,
        attention_gain.reshape(1, width),
        expert_gain.reshape(1, width),
    )
    units = w_gate.shape[1]
    tile = width // TILES
    half_a = capacity * 3 // 5 // 16 * 16
    return pl.pallas_call(
        functools.partial(expert_kernel, half_a),
        out_shape=jax.ShapeDtypeStruct((count, width), BF16),
        in_specs=[vmem] * 3 + [anywhere] * 3,
        out_specs=vmem,
        scratch_shapes=[
            pltpu.VMEM((width, units), BF16),
            pltpu.VMEM((width, units), BF16),
            pltpu.VMEM((units, width), BF16),
            pltpu.VMEM((2, 8, capacity, width), BF16),
            pltpu.VMEM((capacity, width), BF16),
            pltpu.VMEM((8 * capacity, units), BF16),
            pltpu.VMEM((2 * TILES, 8, capacity, tile), BF16),
            pltpu.VMEM((2 * TILES, 4, capacity, tile), BF16),
            pltpu.VMEM((2 * TILES, half_a, tile), BF16),
            pltpu.VMEM((2 * TILES, capacity - half_a, tile), BF16),
            pltpu.VMEM((2 * TILES, capacity, tile), BF16),
            pltpu.VMEM((2 * TILES, capacity, tile), BF16),
            pltpu.VMEM((TILES, capacity, tile), BF16),
            pltpu.VMEM((TILES, capacity, tile), BF16),
            pltpu.VMEM((TILES, capacity, tile), BF16),
            dma((3,)),
            dma((2, 8, TILES)),
            dma((2, 8, TILES)),
            dma((2, TILES)),
            dma((5, 2 * TILES)),
            dma((5, 2 * TILES)),
            dma((TILES,)),
            dma((TILES,)),
        ],
        compiler_params=pltpu.CompilerParams(
            collective_id=1, has_side_effects=True, vmem_limit_bytes=VMEM_BYTES
        ),
    )(ein, after, routed_expert.reshape(1, count), w_gate, w_up, w_down)


def solution(mesh):
    plane = mesh.shape["tensor"] == 1 and mesh.shape["expert"] == 2 * GROUP
    plane = plane and mesh.shape["groups"] == 2
    return jax.shard_map(
        fast_body if plane else body,
        mesh=mesh,
        in_specs=(
            P(("groups", "expert"), None),
            P(("groups", "expert")),
            P(("groups", "expert"), None),
            P(),
            P("expert", "tensor"),
            P("expert", "tensor"),
            P("expert", "tensor"),
            P("expert", "tensor"),
            P(),
            P(None, ("expert", "tensor")),
            P(None, ("expert", "tensor")),
            P(("expert", "tensor"), None),
        ),
        out_specs=P(("groups", "expert"), "tensor"),
        check_vma=False,
    )
```

```python
import functools

import jax
import jax.numpy as jnp
from jax import lax
from jax.experimental import pallas as pl
from jax.experimental.pallas import tpu as pltpu
from jax.sharding import PartitionSpec as P

HEAD = 128
GROUP = 8


def rms_scale(values, gain_vector):
    widened = values.astype(jnp.float32)
    mean_square = jnp.mean(widened * widened, axis=-1, keepdims=True)
    return (widened * lax.rsqrt(mean_square + 1e-05) * gain_vector).astype(jnp.bfloat16)


def slot_numbers(routed, experts, capacity):
    chosen = routed[:, 0]
    one_hot = (chosen[:, None] == jnp.arange(experts, dtype=jnp.int32)[None, :]).astype(jnp.int32)
    running = jnp.cumsum(one_hot, axis=0) - 1
    within = jnp.sum(running * one_hot, axis=1)
    return chosen * capacity + within


def attend(query_rows, key_rows, value_rows, length):
    token_count = query_rows.shape[0]
    head_shape = (token_count, query_rows.shape[1] // HEAD, HEAD)
    scores = jnp.einsum(
        "qhd,khd->hqk",
        query_rows.reshape(head_shape),
        key_rows.reshape(head_shape),
        preferred_element_type=jnp.float32,
    ) * HEAD ** (-0.5)
    positions = jnp.arange(token_count, dtype=jnp.int32)
    allowed = (positions[None, :] <= positions[:, None]) & (positions[None, :] < length)
    scores = jnp.where(allowed[None], scores, -1e30)
    weights = jax.nn.softmax(scores, axis=-1).astype(jnp.bfloat16)
    context = jnp.einsum(
        "hqk,khd->qhd", weights, value_rows.reshape(head_shape), preferred_element_type=jnp.float32
    ).astype(jnp.bfloat16)
    return context.reshape(token_count, -1)


def swiglu_part(arrived_block, gate_weight, up_weight, down_weight):
    gate_sum = jnp.einsum(
        "scd,df->scf", arrived_block, gate_weight, preferred_element_type=jnp.float32
    )
    upward = jnp.einsum("scd,df->scf", arrived_block, up_weight, preferred_element_type=jnp.float32)
    hidden = (jax.nn.silu(gate_sum) * upward).astype(jnp.bfloat16)
    return jnp.einsum("scf,fd->scd", hidden, down_weight, preferred_element_type=jnp.float32)


def body(
    tokens,
    lengths,
    routed_expert,
    attention_gain,
    w_query,
    w_key,
    w_value,
    w_out,
    expert_gain,
    w_gate,
    w_up,
    w_down,
):
    token_count = tokens.shape[0]
    model_width = tokens.shape[1]
    normed = rms_scale(tokens, attention_gain)
    query_sum = jnp.dot(
        normed,
        lax.all_gather(w_query, "expert", axis=0, tiled=True),
        preferred_element_type=jnp.float32,
    )
    key_sum = jnp.dot(
        normed,
        lax.all_gather(w_key, "expert", axis=0, tiled=True),
        preferred_element_type=jnp.float32,
    )
    value_sum = jnp.dot(
        normed,
        lax.all_gather(w_value, "expert", axis=0, tiled=True),
        preferred_element_type=jnp.float32,
    )
    context = attend(
        query_sum.astype(jnp.bfloat16),
        key_sum.astype(jnp.bfloat16),
        value_sum.astype(jnp.bfloat16),
        lengths[0],
    )
    partial_out = lax.dot_general(
        context,
        lax.all_gather(w_out, "expert", axis=0, tiled=True),
        (((1,), (1,)), ((), ())),
        preferred_element_type=jnp.float32,
    )
    cores = lax.axis_size("tensor")
    core_index = lax.axis_index("tensor")
    summed = lax.psum(partial_out, "tensor")
    after_attention = (tokens.astype(jnp.float32) + summed).astype(jnp.bfloat16)
    expert_input = rms_scale(after_attention, expert_gain)
    devices_along = lax.axis_size("expert")
    expert_count = devices_along // GROUP
    capacity = min(token_count, 2 * max(1, 5 * token_count // (8 * expert_count)))
    slot_ids = slot_numbers(routed_expert, expert_count, capacity)
    outgoing_all = (
        jnp.zeros((expert_count * capacity, model_width), jnp.bfloat16)
        .at[slot_ids]
        .set(expert_input)
    )
    outgoing_all = jnp.repeat(
        outgoing_all.reshape(expert_count, capacity, model_width), GROUP, axis=0
    )
    half_width = model_width // cores
    arrived = swiglu_part(
        lax.all_to_all(outgoing_all, "expert", split_axis=0, concat_axis=0, tiled=True),
        w_gate,
        w_up,
        w_down,
    )
    reduced = lax.psum_scatter(arrived, "tensor", scatter_dimension=2, tiled=True).astype(
        jnp.bfloat16
    )
    returned = lax.all_to_all(reduced, "expert", split_axis=0, concat_axis=0, tiled=True)
    part_sums = returned.reshape(expert_count, GROUP, capacity, half_width).astype(jnp.float32)
    expert_rows = jnp.sum(part_sums, axis=1).reshape(expert_count * capacity, half_width)[slot_ids]
    after_half = lax.dynamic_slice_in_dim(after_attention, core_index * half_width, half_width, 1)
    return (after_half.astype(jnp.float32) + expert_rows).astype(jnp.bfloat16)


BF16 = jnp.bfloat16
F32 = jnp.float32
VMEM_BYTES = 60 * 1024 * 1024
TILES = 4


def remote(src, dst, send, recv, target):
    return pltpu.make_async_remote_copy(
        src_ref=src,
        dst_ref=dst,
        send_sem=send,
        recv_sem=recv,
        device_id={"expert": target},
        device_id_type=pl.DeviceIdType.MESH,
    )


def greet(targets):
    barrier = pltpu.get_barrier_semaphore()
    for target in targets:
        pl.semaphore_signal(
            barrier, inc=1, device_id={"expert": target}, device_id_type=pl.DeviceIdType.MESH
        )
    pl.semaphore_wait(barrier, len(targets))


def place():
    me = lax.axis_index("expert")
    core = me % 2
    x = (me // 2) % 2
    z = me // 4
    return me, core, x, z


def gather_kernel(
    lengths,
    tokens,
    w_query,
    w_key,
    w_value,
    w_out,
    gain,
    egain,
    after,
    ein,
    qkv_full,
    out_full,
    normed,
    ctx,
    send,
    recv,
    local,
):
    me, core, x, z = place()
    plane = lax.axis_index("groups")
    shard, heads = w_out.shape
    third = shard // 3
    sib = me + 1 - 2 * core
    across = me + 2 - 4 * x
    fulls = (qkv_full, out_full)

    def rows(who, start, count):
        return pl.ds(pl.multiple_of(who * shard + start, 64), count)

    copies = []
    for k, own in enumerate((w_query, w_key, w_value)):
        into = qkv_full.at[rows(me, 0, shard), pl.ds(k * heads, heads)]
        copies.append(pltpu.make_async_copy(own, into, local.at[k]))
    copies.append(pltpu.make_async_copy(w_out, out_full.at[rows(me, 0, shard)], local.at[3]))
    for copy in copies:
        copy.start()
    barrier = pltpu.get_barrier_semaphore()
    other = {"groups": 1 - plane, "expert": me}
    for target in (sib, across, (me + 4) % 16, (me + 12) % 16):
        pl.semaphore_signal(
            barrier, inc=1, device_id={"expert": target}, device_id_type=pl.DeviceIdType.MESH
        )
    pl.semaphore_signal(barrier, inc=1, device_id=other, device_id_type=pl.DeviceIdType.MESH)
    for copy in copies:
        copy.wait()
    pl.semaphore_wait(barrier, 5)

    targets = (
        {"expert": me + 4},
        {"expert": me - 4},
        {"expert": across},
        {"expert": sib},
        other,
        {"expert": sib},
    )

    def block_of(g, direction, who):
        start, count = third * plane, 2 * third
        if direction == 4:
            start, count = 2 * third * plane, third
        elif direction == 5:
            start, count = 2 * third * (1 - plane), third
        return fulls[g].at[rows(who, start, count)]

    def move(g, direction, who):
        block = block_of(g, direction, who)
        return pltpu.make_async_remote_copy(
            src_ref=block,
            dst_ref=block,
            send_sem=send.at[g, direction, who],
            recv_sem=recv.at[g, direction // 4, who],
            device_id=targets[direction],
            device_id_type=pl.DeviceIdType.MESH,
        )

    def arrived(g, who):
        move(g, 3, who).wait_recv()

    def arrived_third(g, who):
        move(g, 5, who).wait_recv()

    def start(copy):
        copy.start()

    def finish(copy):
        copy.wait_send()

    def each_up(who, act, g):
        @pl.when(z < 3)
        def _():
            act(move(g, 0, who))

    def each_down(who, act, g):
        @pl.when(z > 0)
        def _():
            act(move(g, 1, who))

    def own(g, act):
        each_up(me, act, g)
        each_down(me, act, g)
        act(move(g, 2, me))
        act(move(g, 3, me))
        act(move(g, 5, me))

    def column(g, d, act, wait):
        @pl.when(z >= d)
        def _():
            who = me - 4 * d
            if wait:
                arrived(g, who)
            each_up(who, act, g)
            for direction in (2, 4, 3):
                act(move(g, direction, who))

        @pl.when(z + d <= 3)
        def _():
            who = me + 4 * d
            if wait:
                arrived(g, who)
            each_down(who, act, g)
            for direction in (2, 4, 3):
                act(move(g, direction, who))

    def crossed(g, d, act, wait):
        def pass_on(who):
            if wait:
                arrived(g, who)
            act(move(g, 4, who))
            act(move(g, 3, who))

        if d == 0:
            pass_on(across)
            return

        @pl.when(z >= d)
        def _():
            pass_on(across - 4 * d)

        @pl.when(z + d <= 3)
        def _():
            pass_on(across + 4 * d)

    def thirds(g, d, act, wait):
        def pass_on(who):
            if wait:
                arrived_third(g, who)
            act(move(g, 5, who))

        if d == 0:
            pass_on(across)
            return

        @pl.when(z >= d)
        def _():
            pass_on(me - 4 * d)
            pass_on(across - 4 * d)

        @pl.when(z + d <= 3)
        def _():
            pass_on(me + 4 * d)
            pass_on(across + 4 * d)

    def siblings(g):
        for zz in range(4):
            for xx in range(2):
                arrived(g, (zz * 2 + xx) * 2 + 1 - core)
                arrived_third(g, (zz * 2 + xx) * 2 + 1 - core)

    own(0, start)
    wide = tokens[...].astype(F32)
    mean_square = jnp.mean(wide * wide, axis=-1, keepdims=True)
    normed[...] = (wide * lax.rsqrt(mean_square + 1e-05) * gain[...]).astype(BF16)
    for d in (1, 2, 3):
        column(0, d, start, True)
        crossed(0, d - 1, start, True)
    own(1, start)
    crossed(0, 3, start, True)
    for d in (0, 1, 2, 3):
        thirds(0, d, start, True)
    for d in (1, 2, 3):
        column(1, d, start, True)
        crossed(1, d - 1, start, True)
    siblings(0)

    width = qkv_full.shape[1] // 3
    qkv = jnp.dot(normed[...], qkv_full[...], preferred_element_type=F32).astype(BF16)
    count = tokens.shape[0]
    qpos = lax.broadcasted_iota(jnp.int32, (count, count), 0)
    kpos = lax.broadcasted_iota(jnp.int32, (count, count), 1)
    allowed = (kpos <= qpos) & (kpos < lengths[...])
    for head in range(width // HEAD):
        at = head * HEAD
        query = qkv[:, at : at + HEAD]
        key = qkv[:, width + at : width + at + HEAD]
        value = qkv[:, 2 * width + at : 2 * width + at + HEAD]
        scores = lax.dot_general(
            query, key, (((1,), (1,)), ((), ())), preferred_element_type=F32
        ) * HEAD ** (-0.5)
        scores = jnp.where(allowed, scores, -1e30)
        peak = jnp.max(scores, axis=-1, keepdims=True)
        weights = jnp.exp(scores - peak)
        weights = (weights / jnp.sum(weights, axis=-1, keepdims=True)).astype(BF16)
        ctx[:, at : at + HEAD] = jnp.dot(weights, value, preferred_element_type=F32).astype(BF16)
    crossed(1, 3, start, True)
    for d in (0, 1, 2, 3):
        thirds(1, d, start, True)
    siblings(1)
    attended = lax.dot_general(
        ctx[...], out_full[...], (((1,), (1,)), ((), ())), preferred_element_type=F32
    )
    after[...] = (tokens[...].astype(F32) + attended).astype(BF16)
    wide = after[...].astype(F32)
    mean_square = jnp.mean(wide * wide, axis=-1, keepdims=True)
    ein[...] = (wide * lax.rsqrt(mean_square + 1e-05) * egain[...]).astype(BF16)
    for g in (0, 1):
        own(g, finish)
        for d in (0, 1, 2, 3):
            if d:
                column(g, d, finish, False)
            crossed(g, d, finish, False)
            thirds(g, d, finish, False)


def expert_kernel(
    half_a,
    ein,
    after,
    routed,
    w_gate,
    w_up,
    w_down,
    out,
    gate_v,
    up_v,
    down_v,
    rows_in,
    far_own,
    gate_sum,
    up_sum,
    hidden,
    part,
    from_sib,
    diag_x,
    diag_z,
    sum_x,
    sum_z,
    near_sum,
    far_sum,
    far_back,
    wsem,
    gsend,
    grecv,
    csem,
    rsend,
    rrecv,
    fsend,
    frecv,
):
    me, core, x, z = place()
    near = z // 2
    sib = me + 1 - 2 * core
    across = me + 2 - 4 * x
    along = me + 4 - 8 * (z % 2)
    mirror = me + 12 - 8 * z
    slots, cap, width = rows_in.shape[1], rows_in.shape[2], rows_in.shape[3]
    loads = []
    for k, (src, dst) in enumerate(((w_gate, gate_v), (w_up, up_v), (w_down, down_v))):
        copy = pltpu.make_async_copy(src, dst, wsem.at[k])
        copy.start()
        loads.append(copy)
    count = ein.shape[0]
    chosen = routed[...]
    earlier = lax.broadcasted_iota(jnp.int32, (count, count), 0) <= lax.broadcasted_iota(
        jnp.int32, (count, count), 1
    )

    def slot_matrix(expert):
        named = jnp.broadcast_to(chosen == expert, (16, count))
        number = jnp.dot(
            named.astype(BF16), earlier.astype(BF16), preferred_element_type=F32
        ).astype(jnp.int32)[0:1]
        slot = lax.broadcasted_iota(jnp.int32, (cap, count), 0) + 1
        return ((slot == number) & (chosen == expert)).astype(BF16)

    far_pick = slot_matrix(1 - near)
    near_pick = slot_matrix(near)
    far_own[...] = jnp.dot(far_pick, ein[...], preferred_element_type=F32).astype(BF16)
    rows_in[0, 0] = jnp.dot(near_pick, ein[...], preferred_element_type=F32).astype(BF16)
    greet((sib, across, along, mirror))

    fan = gate_v.shape[1] // TILES
    tile = width // TILES

    def columns(t):
        return pl.ds(pl.multiple_of(t * tile, tile), tile)

    def gathering(kind, k, t):
        cut = (half_a + 16, half_a)[k]
        every, lower, upper = pl.ds(0, cap), pl.ds(0, cut), pl.ds(cut, cap - cut)
        source, slot, rows, target = (
            (0, 1, every, across),
            (0, 2, every, along),
            (0, 4, every, sib),
            (1, 3, upper, along),
            (1, 5, every, sib),
            (2, 3, lower, across),
            (2, 6, every, sib),
            (3, 7, every, sib),
        )[kind]
        return remote(
            rows_in.at[k, source, rows, columns(t)],
            rows_in.at[k, slot, rows, columns(t)],
            gsend.at[k, kind, t],
            grecv.at[k, kind, t],
            target,
        )

    def crossing(t):
        return remote(
            far_own.at[:, columns(t)],
            rows_in.at[1, 0, :, columns(t)],
            csem.at[0, t],
            csem.at[1, t],
            mirror,
        )

    def gather_own(k, t):
        for kind in (0, 1, 2):
            gathering(kind, k, t).start()

    def gather_pass(k, t):
        gathering(0, k, t).wait_recv()
        gathering(3, k, t).start()
        gathering(4, k, t).start()
        gathering(1, k, t).wait_recv()
        gathering(5, k, t).start()
        gathering(6, k, t).start()

    def gather_last(k, t):
        gathering(3, k, t).wait_recv()
        gathering(5, k, t).wait_recv()
        gathering(7, k, t).start()

    def gather_done(k, t):
        for kind in (2, 4, 6, 7):
            gathering(kind, k, t).wait_recv()

    def up_part(k, t):
        given = rows_in[k, :, :, columns(t)].reshape(slots * cap, tile)

        def block(j, c):
            cols = pl.ds(pl.multiple_of(j * fan, fan), fan)
            gate = jnp.dot(given, gate_v[columns(t), cols], preferred_element_type=F32)
            upward = jnp.dot(given, up_v[columns(t), cols], preferred_element_type=F32)

            @pl.when(t == 0)
            def _():
                gate_sum[:, cols] = gate
                up_sum[:, cols] = upward

            @pl.when(t > 0)
            def _():
                gate_sum[:, cols] += gate
                up_sum[:, cols] += upward

            return c

        lax.fori_loop(0, TILES, block, 0)

    def activate(t):
        cols = pl.ds(pl.multiple_of(t * fan, fan), fan)
        hidden[:, cols] = (jax.nn.silu(gate_sum[:, cols]) * up_sum[:, cols]).astype(BF16)

    def down_tile(k, t):
        cols = columns(t)
        total = jnp.dot(hidden[...], down_v[:, cols], preferred_element_type=F32)
        part[k * TILES + t] = total.astype(BF16).reshape(slots, cap, tile)

    def summing(kind, i):
        rest = cap - half_a
        ends = (
            (part.at[i, pl.ds(4, 4)], from_sib.at[i], sib),
            (part.at[i, 3, pl.ds(0, half_a)], diag_x.at[i], across),
            (part.at[i, 3, pl.ds(half_a, rest)], diag_z.at[i], along),
            (part.at[i, 1], sum_x.at[i], across),
            (part.at[i, 2], sum_z.at[i], along),
        )[kind]
        return remote(ends[0], ends[1], rsend.at[kind, i], rrecv.at[kind, i], ends[2])

    def plus(a, b):
        return (a.astype(F32) + b.astype(F32)).astype(BF16)

    def step_core(i):
        summing(0, i).wait_recv()
        part[i, 3] = plus(part[i, 3], from_sib[i, 3])
        summing(1, i).start()
        summing(2, i).start()
        part[i, 0:3] = plus(part[i, 0:3], from_sib[i, 0:3])

    def step_diag(i):
        summing(1, i).wait_recv()
        part[i, 2, 0:half_a] = plus(part[i, 2, 0:half_a], diag_x[i])
        summing(4, i).start()
        summing(2, i).wait_recv()
        part[i, 1, half_a:cap] = plus(part[i, 1, half_a:cap], diag_z[i])
        summing(3, i).start()

    def total_of(i):
        summing(3, i).wait_recv()
        summing(4, i).wait_recv()
        total = part[i, 0].astype(F32) + sum_x[i].astype(F32) + sum_z[i].astype(F32)
        return total.astype(BF16)

    def returning(t):
        return remote(far_sum.at[t], far_back.at[t], fsend.at[t], frecv.at[t], mirror)

    def loop(body):
        lax.fori_loop(0, TILES, lambda t, c: (body(t), c)[1], 0)

    def begin(t):
        gather_own(0, t)
        crossing(t).start()

    def second(t):
        gather_pass(0, t)
        crossing(t).wait_recv()
        gather_own(1, t)

    loop(begin)
    loop(second)
    loop(functools.partial(gather_last, 0))
    for copy in loads:
        copy.wait()

    def near_up(t):
        gather_done(0, t)
        up_part(0, t)
        gather_pass(1, t)

    loop(near_up)
    loop(activate)

    def near_down(t):
        down_tile(0, t)
        summing(0, t).start()
        gather_last(1, t)

        @pl.when(t > 0)
        def _():
            step_core(t - 1)

    loop(near_down)
    step_core(TILES - 1)
    def far_up(t):
        gather_done(1, t)
        up_part(1, t)
        step_diag(t)

    loop(far_up)
    loop(activate)

    def far_steps(t, c):
        i = TILES + t

        @pl.when(t < TILES)
        def _():
            down_tile(1, t)
            summing(0, i).start()
            near_sum[t] = total_of(t)

        @pl.when((t >= 1) & (t < TILES + 1))
        def _():
            step_core(i - 1)

        @pl.when((t >= 2) & (t < TILES + 2))
        def _():
            step_diag(i - 2)

        @pl.when(t >= 3)
        def _():
            far_sum[t - 3] = total_of(i - 3)
            returning(t - 3).start()

        return c

    lax.fori_loop(0, TILES + 3, far_steps, 0)

    def finish(t):
        cols = columns(t)
        returning(t).wait_recv()
        first = (((0,), (0,)), ((), ()))
        moved = lax.dot_general(near_pick, near_sum[t], first, preferred_element_type=F32)
        moved = moved + lax.dot_general(far_pick, far_back[t], first, preferred_element_type=F32)
        out[:, cols] = (after[:, cols].astype(F32) + moved).astype(BF16)

    loop(finish)

    def drain_gather(t):
        returning(t).wait_send()
        crossing(t).wait_send()
        for k in range(2):
            for kind in range(8):
                gathering(kind, k, t).wait_send()

    loop(drain_gather)

    def drain(i, c):
        for kind in range(5):
            summing(kind, i).wait_send()
        return c

    lax.fori_loop(0, 2 * TILES, drain, 0)


def fast_body(
    tokens,
    lengths,
    routed_expert,
    attention_gain,
    w_query,
    w_key,
    w_value,
    w_out,
    expert_gain,
    w_gate,
    w_up,
    w_down,
):
    count, width = tokens.shape
    devices = lax.axis_size("expert")
    experts = devices // GROUP
    capacity = min(count, 2 * max(1, 5 * count // (8 * experts)))
    vmem = pl.BlockSpec(memory_space=pltpu.VMEM)
    anywhere = pl.BlockSpec(memory_space=pl.ANY)
    heads = w_query.shape[1]
    dma = pltpu.SemaphoreType.DMA
    after, ein = pl.pallas_call(
        gather_kernel,
        out_shape=[jax.ShapeDtypeStruct((count, width), BF16)] * 2,
        in_specs=[vmem] * 2 + [anywhere] * 4 + [vmem] * 2,
        out_specs=[vmem] * 2,
        scratch_shapes=[
            pltpu.VMEM((width, 3 * heads), BF16),
            pltpu.VMEM((width, heads), BF16),
            pltpu.VMEM((count, width), BF16),
            pltpu.VMEM((count, heads), BF16),
            dma((2, 6, devices)),
            dma((2, 2, devices)),
            dma((4,)),
        ],
        compiler_params=pltpu.CompilerParams(
            collective_id=0, has_side_effects=True, vmem_limit_bytes=VMEM_BYTES
        ),
    )(
        lengths.reshape(1, 1),
        tokens,
        w_query,
        w_key,
        w_value,
        w_out,
        attention_gain.reshape(1, width),
        expert_gain.reshape(1, width),
    )
    units = w_gate.shape[1]
    tile = width // TILES
    half_a = capacity * 3 // 5 // 16 * 16
    return pl.pallas_call(
        functools.partial(expert_kernel, half_a),
        out_shape=jax.ShapeDtypeStruct((count, width), BF16),
        in_specs=[vmem] * 3 + [anywhere] * 3,
        out_specs=vmem,
        scratch_shapes=[
            pltpu.VMEM((width, units), BF16),
            pltpu.VMEM((width, units), BF16),
            pltpu.VMEM((units, width), BF16),
            pltpu.VMEM((2, 8, capacity, width), BF16),
            pltpu.VMEM((capacity, width), BF16),
            pltpu.VMEM((8 * capacity, units), F32),
            pltpu.VMEM((8 * capacity, units), F32),
            pltpu.VMEM((8 * capacity, units), BF16),
            pltpu.VMEM((2 * TILES, 8, capacity, tile), BF16),
            pltpu.VMEM((2 * TILES, 4, capacity, tile), BF16),
            pltpu.VMEM((2 * TILES, half_a, tile), BF16),
            pltpu.VMEM((2 * TILES, capacity - half_a, tile), BF16),
            pltpu.VMEM((2 * TILES, capacity, tile), BF16),
            pltpu.VMEM((2 * TILES, capacity, tile), BF16),
            pltpu.VMEM((TILES, capacity, tile), BF16),
            pltpu.VMEM((TILES, capacity, tile), BF16),
            pltpu.VMEM((TILES, capacity, tile), BF16),
            dma((3,)),
            dma((2, 8, TILES)),
            dma((2, 8, TILES)),
            dma((2, TILES)),
            dma((5, 2 * TILES)),
            dma((5, 2 * TILES)),
            dma((TILES,)),
            dma((TILES,)),
        ],
        compiler_params=pltpu.CompilerParams(
            collective_id=1, has_side_effects=True, vmem_limit_bytes=VMEM_BYTES
        ),
    )(ein, after, routed_expert.reshape(1, count), w_gate, w_up, w_down)


def solution(mesh):
    plane = mesh.shape["tensor"] == 1 and mesh.shape["expert"] == 2 * GROUP
    plane = plane and mesh.shape["groups"] == 2
    return jax.shard_map(
        fast_body if plane else body,
        mesh=mesh,
        in_specs=(
            P(("groups", "expert"), None),
            P(("groups", "expert")),
            P(("groups", "expert"), None),
            P(),
            P("expert", "tensor"),
            P("expert", "tensor"),
            P("expert", "tensor"),
            P("expert", "tensor"),
            P(),
            P(None, ("expert", "tensor")),
            P(None, ("expert", "tensor")),
            P(("expert", "tensor"), None),
        ),
        out_specs=P(("groups", "expert"), "tensor"),
        check_vma=False,
    )
```
